32 devices in a mesh: gx: 2 (over x), gy: 4 (over y, core), gz: 4 (over z).
Axes of the slice: x: 2, y: 2, z: 4, core: 2. Of those that a mesh axis runs over, the one named last changes fastest.
Arguments:
- source: float32 [32, 128, 512], P('gx', 'gy', 'gz'), may hold values from -24 to 24
- conductivity: float32 [32, 128, 512], P('gx', 'gy', 'gz'), may hold values from 0.5 to 8
Outputs:
- correction: float32 [32, 128, 512], P('gx', 'gy', 'gz')
The draws below stay inside these ranges and needn't reach their ends.
All inputs are finite; a program needn't handle non-finite values.
Results may differ from the reference program's by a relative error of at most 0.0001.
Values sent between devices are 32-bit elements; how exact they have to be, the bound alone decides.
No kernel may reach another device: no remote copies, remote signals or barrier semaphores. Data moves between devices by JAX's collectives and lax.ppermute only.
A program may use at most 128 MiB of HBM per device.

```python
import math
import jax
import jax.numpy as jnp
from jax import lax

SWEEPS = 6
COARSE_SWEEPS = 16
NX = 32
NY = 128
NZ = 512


def steps_of(stream_key, extent, shards, least, top_value):
    loudness = 1.0
    for axis_at, blocks in shards:
        draws = jax.random.uniform(jax.random.fold_in(jax.random.fold_in(stream_key, 6), axis_at), (blocks,), jnp.float32, least / len(shards), top_value / len(shards))
        loudness = loudness * jnp.repeat(jnp.exp(draws), extent[axis_at] // blocks).reshape((-1,) + (1,) * (len(extent) - 1 - axis_at))
    return loudness


def normal_values(stream_key, dims, deviation, limit, pieces=(), held_as=jnp.bfloat16):
    gain = steps_of(stream_key, dims, pieces, -0.22, 0.18) if pieces else 1.0
    values = jax.random.normal(stream_key, dims, jnp.float32) * deviation * gain
    return jnp.minimum(jnp.maximum(values, -limit), limit).astype(held_as)


def setup_inputs(seed: int = 0) -> dict:
    seeds = jax.random.split(jax.random.key(seed), 3)
    return {
        "source": normal_values(seeds[0], (NX, NY, NZ), 4.0, 24.0, ((0, 2), (1, 4), (2, 4)), jnp.float32),
        "conductivity": jnp.clip(jnp.exp(math.log(8.0) - 2.7725887 * jax.random.uniform(seeds[1], (NX, NY, NZ), jnp.float32) ** steps_of(seeds[1], (NX, NY, NZ), ((0, 2), (1, 4), (2, 4)), -0.2, 0.2)), 0.5, 8.0),
    }


DAMPING = 0.8


def centre(padded):
    return padded[1:-1, 1:-1, 1:-1]


def neighbours(padded):
    return [padded[2:, 1:-1, 1:-1], padded[:-2, 1:-1, 1:-1], padded[1:-1, 2:, 1:-1],
            padded[1:-1, :-2, 1:-1], padded[1:-1, 1:-1, 2:], padded[1:-1, 1:-1, :-2]]


def zero_pad(field):
    return jnp.pad(field, 1)


def stencil(field_pad, coef_pad, weight):
    middle = centre(field_pad)
    coef_mid = centre(coef_pad)
    total = jnp.zeros_like(middle)
    for field_near, coef_near in zip(neighbours(field_pad), neighbours(coef_pad)):
        total = total + 0.5 * (coef_mid + coef_near) * (middle - field_near)
    return weight * total


def diagonal(coef_pad, weight):
    coef_mid = centre(coef_pad)
    total = jnp.zeros_like(coef_mid)
    for coef_near in neighbours(coef_pad):
        total = total + 0.5 * (coef_mid + coef_near)
    return weight * total


def restrict(field):
    shape = field.shape
    blocks = field.reshape(shape[0] // 2, 2, shape[1] // 2, 2, shape[2] // 2, 2)
    return blocks.mean(axis=(1, 3, 5))


def prolong(field):
    return jnp.repeat(jnp.repeat(jnp.repeat(field, 2, 0), 2, 1), 2, 2)


def jacobi(field, rhs_level, coef_pad, diag_terms, weight, padder):
    return field + DAMPING * (rhs_level - stencil(padder(field), coef_pad, weight)) / diag_terms


def reference(source, conductivity):
    rhs_level = source
    coef_level = conductivity
    saved = []
    for level_index in range(4):
        weight = 0.25 ** level_index
        coef_pad = zero_pad(coef_level)
        diag_terms = diagonal(coef_pad, weight)
        field = jnp.zeros_like(rhs_level)
        for sweep_index in range(SWEEPS):
            field = jacobi(field, rhs_level, coef_pad, diag_terms, weight, zero_pad)
        residual = rhs_level - stencil(zero_pad(field), coef_pad, weight)
        saved.append((field, rhs_level, coef_pad, diag_terms, weight))
        rhs_level = restrict(residual)
        coef_level = restrict(coef_level)
    weight = 0.25 ** 4
    coef_pad = zero_pad(coef_level)
    diag_terms = diagonal(coef_pad, weight)

    def coarse_step(count, field):
        return jacobi(field, rhs_level, coef_pad, diag_terms, weight, zero_pad)

    result = lax.fori_loop(0, COARSE_SWEEPS, coarse_step, jnp.zeros_like(rhs_level))
    for level_index in (3, 2, 1, 0):
        field, rhs_here, coef_pad, diag_terms, weight = saved[level_index]
        field = field + prolong(result)
        for sweep_index in range(SWEEPS):
            field = jacobi(field, rhs_here, coef_pad, diag_terms, weight, zero_pad)
        result = field
    return result
```

```python
import functools

import jax
import jax.numpy as jnp
from jax import lax
from jax.experimental import pallas as pl
from jax.experimental.pallas import tpu as pltpu
from jax.sharding import PartitionSpec as P

SWEEPS = 6
COARSE_SWEEPS = 16
DAMPING = 0.8
VMEM_BYTES = 32 * 2**20


def with_halo(array, sides, width):
    for axis, dim in sides:
        size, length = (lax.axis_size(axis), array.shape[dim])
        up = [(i, (i + 1) % size) for i in range(size - 1)]
        down = [(j, i) for i, j in up]
        last = lax.slice_in_dim(array, length - width, length, axis=dim)
        first = lax.slice_in_dim(array, 0, width, axis=dim)
        before = lax.ppermute(last, axis, up)
        after = lax.ppermute(first, axis, down)
        array = jnp.concatenate([before, array, after], axis=dim)
    return array


def centre(padded):
    return padded[1:-1, 1:-1, 1:-1]


def neighbours(padded):
    return [
        padded[2:, 1:-1, 1:-1],
        padded[:-2, 1:-1, 1:-1],
        padded[1:-1, 2:, 1:-1],
        padded[1:-1, :-2, 1:-1],
        padded[1:-1, 1:-1, 2:],
        padded[1:-1, 1:-1, :-2],
    ]


def zero_pad(field):
    return jnp.pad(field, 1)


def stencil(field_pad, coef_pad, weight):
    middle = centre(field_pad)
    coef_mid = centre(coef_pad)
    total = jnp.zeros_like(middle)
    for field_near, coef_near in zip(neighbours(field_pad), neighbours(coef_pad)):
        total = total + 0.5 * (coef_mid + coef_near) * (middle - field_near)
    return weight * total


def diagonal(coef_pad, weight):
    coef_mid = centre(coef_pad)
    total = jnp.zeros_like(coef_mid)
    for coef_near in neighbours(coef_pad):
        total = total + 0.5 * (coef_mid + coef_near)
    return weight * total


def restrict(field):
    shape = field.shape
    blocks = field.reshape(shape[0] // 2, 2, shape[1] // 2, 2, shape[2] // 2, 2)
    return blocks.mean(axis=(1, 3, 5))


def prolong(field):
    return jnp.repeat(jnp.repeat(jnp.repeat(field, 2, 0), 2, 1), 2, 2)


def jacobi(field, rhs_level, coef_pad, diag_terms, weight, padder):
    return field + DAMPING * (rhs_level - stencil(padder(field), coef_pad, weight)) / diag_terms


def face_rim(field):
    return with_halo(field, (("gx", 0), ("gy", 1), ("gz", 2)), 1)


def slab_pad(field):
    extended = with_halo(field, (("gx", 0),), 1)
    return jnp.pad(extended, ((0, 0), (1, 1), (1, 1)))


def single_sweeps(field, rhs_level, coef_pad, diag_terms, weight):
    for sweep_index in range(SWEEPS):
        field = jacobi(field, rhs_level, coef_pad, diag_terms, weight, face_rim)
    return field


def coarse_solve(rhs_level, coef_level):
    weight = 0.25**4
    coef_pad = zero_pad(coef_level)
    diag_terms = diagonal(coef_pad, weight)

    def coarse_step(count, field):
        return jacobi(field, rhs_level, coef_pad, diag_terms, weight, zero_pad)

    return lax.fori_loop(0, COARSE_SWEEPS, coarse_step, jnp.zeros_like(rhs_level))


def level_three(rhs_level, coef_level, padder, lower_solve):
    weight = 0.25**3
    coef_pad = padder(coef_level)
    diag_terms = diagonal(coef_pad, weight)
    field = jnp.zeros_like(rhs_level)
    for sweep_index in range(SWEEPS):
        field = jacobi(field, rhs_level, coef_pad, diag_terms, weight, padder)
    residual = rhs_level - stencil(padder(field), coef_pad, weight)
    field = field + prolong(lower_solve(restrict(residual), restrict(coef_level)))
    for sweep_index in range(SWEEPS):
        field = jacobi(field, rhs_level, coef_pad, diag_terms, weight, padder)
    return field


def plain_shards(source, conductivity):
    count_x, count_y, count_z = (lax.axis_size("gx"), lax.axis_size("gy"), lax.axis_size("gz"))
    place_x, place_y, place_z = (lax.axis_index("gx"), lax.axis_index("gy"), lax.axis_index("gz"))
    rhs_level = source
    coef_level = conductivity
    saved = []
    for level_index in range(3):
        weight = 0.25**level_index
        coef_pad = face_rim(coef_level)
        diag_terms = diagonal(coef_pad, weight)
        extras = None
        field = single_sweeps(jnp.zeros_like(rhs_level), rhs_level, coef_pad, diag_terms, weight)
        residual = rhs_level - stencil(face_rim(field), coef_pad, weight)
        saved.append((field, rhs_level, coef_pad, diag_terms, weight, extras))
        rhs_level = restrict(residual)
        coef_level = restrict(coef_level)
    rows_x, rows_y, rows_z = rhs_level.shape
    stacked = jnp.stack([rhs_level, coef_level])[None]
    gathered = lax.all_gather(stacked, ("gy", "gz"), axis=0, tiled=True)
    slab = gathered.reshape(count_y, count_z, 2, rows_x, rows_y, rows_z)
    slab = slab.transpose(2, 3, 0, 4, 1, 5).reshape(2, rows_x, count_y * rows_y, count_z * rows_z)

    def lower_groups(rhs_low, coef_low):
        lowered = lax.all_gather(jnp.stack([rhs_low, coef_low]), "gx", axis=1, tiled=True)
        whole = coarse_solve(lowered[0], lowered[1])
        return lax.dynamic_slice_in_dim(whole, place_x * (rows_x // 2), rows_x // 2, 0)

    field = level_three(slab[0], slab[1], slab_pad, lower_groups)
    field = lax.dynamic_slice_in_dim(field, place_y * rows_y, rows_y, 1)
    result = lax.dynamic_slice_in_dim(field, place_z * rows_z, rows_z, 2)
    for level_index in (2, 1, 0):
        field, rhs_here, coef_pad, diag_terms, weight, extras = saved[level_index]
        field = field + prolong(result)
        field = single_sweeps(field, rhs_here, coef_pad, diag_terms, weight)
        result = field
    return result


ROWS = 48
MARGIN = 8
MAIN = MARGIN + 25 * ROWS + MARGIN
STRIP = MARGIN + 5 * ROWS + MARGIN
SECOND = MARGIN + 18 * ROWS + MARGIN


def roll(value, shift, axis):
    if isinstance(shift, int):
        shift = shift % value.shape[axis]
        if shift == 0:
            return value
    return pltpu.roll(value, shift, axis)


def iota(shape, axis):
    return lax.broadcasted_iota(jnp.int32, shape, axis)


def gather_lanes(value, lanes):
    return jnp.take_along_axis(value, lanes, axis=1, mode="promise_in_bounds")


def block(at, count):
    return pl.ds(pl.multiple_of(at, 8) if not isinstance(at, int) else at, count)


def terms(coef, nears, rhs, weight):
    faces = [0.5 * (coef + near) for near in nears]
    total = functools.reduce(lambda a, b: a + b, faces)
    scale = jnp.where(coef > 0.0, DAMPING / total, 0.0)
    return faces, scale, rhs * scale * (1.0 / weight), total * (weight / DAMPING)


def each(count, body, step):
    def several(turn, carry):
        for ahead in range(step):
            body(turn * step + ahead)
        return carry

    def single(index, carry):
        body(index)
        return carry

    whole = count // step
    lax.fori_loop(0, whole, several, 0)
    if count % step:
        lax.fori_loop(whole * step, count, single, 0)


def row_pairs(array, rows):
    return array[pl.ds(0, rows // 2, stride=2), :] + array[pl.ds(1, rows // 2, stride=2), :]


def repeat_rows(array, value):
    rows = value.shape[0]
    array[pl.ds(0, rows, stride=2), :] = value
    array[pl.ds(1, rows, stride=2), :] = value


def lane_pairs(value):
    return value + roll(value, -1, 1)


def both_ways(face, value, axis):
    return face * roll(value, -1, axis) + roll(face * value, 1, axis)


def by_side(swapped, odd):
    first, second = swapped
    return jnp.where(odd, first, second), jnp.where(odd, second, first)


def device_place():
    return [lax.axis_index(axis) for axis in ("gx", "gy", "gz")]


def odd_at(place, axis):
    return (place[axis] & 1) == 1


def with_tiles(middle, first, second, odd):
    sides = [by_side(tiles, odd) for tiles in zip(first, second)]
    return jnp.concatenate([low for low, _ in sides] + list(middle) + [high for _, high in sides], axis=0)


def main_at(plane):
    return MARGIN + ROWS * plane


def joined(middle, edge):
    lane = iota(middle.shape, 1)
    return jnp.where(lane == 127, edge, roll(middle, -1, 1)), jnp.where(lane == 0, edge, roll(middle, 1, 1))


def facing(own, plane, slot):
    lane = iota(own.shape, 1)
    return jnp.where((lane == 16 * slot + 7) | (lane == 16 * slot + 8), roll(plane, 16 * slot + 8, 1), own)


def strip_nears(strip, own, group):
    at = main_at(group + 1)
    middle = strip[block(at, ROWS)]
    lane = iota((ROWS, 128), 1)
    slot_lane = lane & 15
    further = jnp.where(lane < 112, roll(middle, -16, 1), roll(strip[block(at + ROWS, ROWS)], -16, 1))
    nearer = jnp.where(lane >= 16, roll(middle, 16, 1), roll(strip[block(at - ROWS, ROWS)], 16, 1))
    after = jnp.where(slot_lane == 7, own, roll(middle, -1, 1))
    before = jnp.where(slot_lane == 8, own, roll(middle, 1, 1))
    return middle, [further, nearer, roll(middle, -1, 0), roll(middle, 1, 0), after, before]


def finest_terms(rhs, coef, kept, inverse):
    main, strip = coef

    def group(index, slots):
        first = 8 * index + 1
        before = main[block(main_at(first - 1), ROWS)]
        here = main[block(main_at(first), ROWS)]
        held = strip[block(main_at(index + 1), ROWS)]
        own = jnp.zeros((ROWS, 128), jnp.float32)
        for slot in range(slots):
            at = block(main_at(first + slot), ROWS)
            after = main[block(main_at(first + slot + 1), ROWS)]
            nears = [after, before, roll(here, -1, 0), roll(here, 1, 0), *joined(here, roll(held, 120 - 16 * slot, 1))]
            faces, scale, start, back = terms(here, nears, rhs[0][at], 1.0)
            for side, value in enumerate((faces[0], faces[2], faces[4], faces[5], scale, start)):
                kept[0][side, at] = value
            inverse[at] = back
            own = facing(own, here, slot)
            before, here = here, after
        for slot in range(slots, 8):
            own = facing(own, main[block(main_at(first + slot), ROWS)], slot)
        at = block(main_at(index + 1), ROWS)
        middle, nears = strip_nears(strip, own, index)
        faces, scale, start, _ = terms(middle, nears, rhs[1][at], 1.0)
        for side in range(6):
            kept[1][side, at] = faces[side] * scale
        kept[1][6, at] = start

    each(2, lambda index: group(index, 8), 1)
    group(2, 6)


def finest_sweep(count, kept, source, target, keep=1.0 - DAMPING, strips=True):
    main, strip = source

    def group(index, slots):
        first = 8 * index + 1
        at = block(main_at(first - 1), ROWS)
        flux = kept[0][0, at] * main[at]
        here = main[block(main_at(first), ROWS)]
        held = strip[block(main_at(index + 1), ROWS)]
        own = jnp.zeros((ROWS, 128), jnp.float32)
        for slot in range(slots):
            at = block(main_at(first + slot), ROWS)
            after = main[block(main_at(first + slot + 1), ROWS)]
            face = kept[0][0, at]
            total = flux + face * after
            flux = face * here
            total = total + both_ways(kept[0][1, at], here, 0)
            above, below = joined(here, roll(held, 120 - 16 * slot, 1))
            total = total + kept[0][2, at] * above + kept[0][3, at] * below
            target[0][at] = kept[0][5, at] + keep * here + kept[0][4, at] * total
            if strips:
                own = facing(own, here, slot)
            here = after
        if strips:
            at = block(main_at(index + 1), ROWS)
            middle, nears = strip_nears(strip, own, index)
            total = kept[1][6, at] + keep * middle
            for side, near in enumerate(nears):
                total = total + kept[1][side, at] * near
            target[1][at] = total

    each(2, lambda index: group(index, 8), 1)
    if count > 16:
        group(2, count - 16)


def strip_pages(rhs_planes, coef_planes):
    lane = iota((32, 128), 1)
    left = jnp.zeros((32, 128), jnp.float32)
    right = jnp.zeros((32, 128), jnp.float32)
    for field_at, planes in ((0, rhs_planes), (8, coef_planes)):
        for slot, plane in enumerate(planes):
            at = 16 * slot + field_at
            inside = (lane >= at) & (lane < at + 8)
            left = jnp.where(inside, gather_lanes(plane, 7 - (lane & 7)), left)
            right = jnp.where(inside, gather_lanes(plane, 127 - (lane & 7)), right)
    return left, right


def plane_kernel(rhs, coef, fields, message):
    side = lax.axis_index("gx")
    for field_at, array in enumerate((rhs, coef)):
        for local in range(16):
            plane = array[local + side * (15 - 2 * local)]
            fields[16 * field_at + local] = plane
            if local > 9 - field_at:
                message[6 * field_at + 15 - local] = plane


def edge_kernel(fields, to_first, to_second, rows_first, rows_second):
    place = device_place()
    odd, odd_y = odd_at(place, 2), odd_at(place, 1)
    for group in range(2):
        planes = [[fields[16 * field_at + 8 * group + slot] for slot in range(8)] for field_at in range(2)]
        to_first[group], to_second[group] = by_side(strip_pages(*planes), odd)
    for page in range(32):
        rows_first[page], rows_second[page] = by_side((fields[page, 0:8], fields[page, 24:32]), odd_y)


def mirrored_slots(value):
    lane = iota(value.shape, 1)
    found = value
    for slot in range(8):
        inside = (lane >= 16 * slot) & (lane < 16 * slot + 16)
        found = jnp.where(inside, roll(value, 16 * (2 * slot - 7), 1), found)
    return found


def finest_kernel(own, strips, own_first, own_second, strip_first, strip_second, partner, beside, corner, pre, lower, message,
                  to_first, to_second, kept, kept_strip, rhs, rhs_strip, coef, coef_strip, va, va_strip, vb, vb_strip, inverse,
                  sums):
    place = device_place()
    blank = jnp.zeros((ROWS, 128), jnp.float32)
    outside = block(main_at(0), ROWS)
    for array in (coef, va, vb):
        array[outside] = blank
    coef[block(main_at(24), ROWS)] = blank
    kept[0, outside] = blank
    kept[5, outside] = blank
    for array in (coef_strip, va_strip, vb_strip, kept_strip.at[6]):
        array[outside] = blank
        array[block(main_at(4), ROWS)] = blank
    odd_y, odd_z = odd_at(place, 1), odd_at(place, 2)

    no_rows = jnp.zeros((8, 128), jnp.float32)
    for local in range(23):
        at = block(main_at(local + 1), ROWS)
        for field_at, array in enumerate((rhs, coef)):
            if local < 16:
                page = 16 * field_at + local
                array[at] = with_tiles([own[page]], [own_first[page]], [own_second[page]], odd_y)
            elif local < 22 + field_at:
                step = local - 16
                page = 12 + 6 * field_at - step
                beyond = step == 5 + field_at
                first, second = (no_rows, no_rows) if beyond else (beside[page], beside[11 + page])
                array[at] = with_tiles([partner[6 * field_at + step]], [first], [second], odd_y)
    above = (iota((ROWS, 128), 1) & 15) < 8
    for group in range(3):
        pages = []
        for which in range(2):
            if group < 2:
                page = 2 - 2 * which + group
                pages.append(with_tiles([strips[page]], [strip_first[page]], [strip_second[page]], odd_y))
            else:
                tiles = [beside[4 - 4 * which + part] for part in range(4)]
                pages.append(with_tiles(tiles, [corner[1 - which]], [corner[3 - which]], odd_y))
        left, right = by_side(pages, odd_z)
        if group == 2:
            left, right = mirrored_slots(left), mirrored_slots(right)
        at = block(main_at(group + 1), ROWS)
        rhs_strip[at] = jnp.where(above, right, roll(left, 8, 1))
        coef_strip[at] = jnp.where(above, roll(right, -8, 1), left)
    both = (kept, kept_strip)
    finest_terms((rhs, rhs_strip), (coef, coef_strip), both, inverse)
    a, b = (va, va_strip), (vb, vb_strip)
    source = (kept.at[5], kept_strip.at[6])
    for count, target in zip(range(21, 16, -1), (a, b, a, b, a)):
        finest_sweep(count, both, source, target)
        source = target
    finest_sweep(16, both, a, b, -DAMPING, False)

    def pair(index):
        total = jnp.zeros((32, 128), jnp.float32)
        conduct = jnp.zeros((32, 128), jnp.float32)
        for local in (2 * index, 2 * index + 1):
            at = block(main_at(local + 1) + 8, 32)
            value = va[at]
            pre[local] = value
            total = total + vb[at] * inverse[at]
            conduct = conduct + coef[at]
        sums[block(index * 32, 32)] = total
        sums[block(index * 32 + 256, 32)] = conduct

    each(8, pair, 4)
    folded = lane_pairs(row_pairs(sums, 512)) * 0.125
    lane = iota((128, 128), 1)
    merged = jnp.where(lane < 64, gather_lanes(folded[0:128], (2 * lane) & 127), gather_lanes(folded[128:256], (2 * lane) & 127))
    lane = iota((16, 128), 1)
    for group in range(2):
        right = jnp.zeros((16, 128), jnp.float32)
        left = jnp.zeros((16, 128), jnp.float32)
        for slot in range(4):
            local = 4 * group + slot
            plane = merged[16 * local : 16 * local + 16]
            lower[local] = plane
            message[2 * local] = plane[0:8]
            message[2 * local + 1] = plane[8:16]
            for field_at in range(2):
                at = 32 * slot + 16 * field_at
                inside = (lane >= at) & (lane < at + 16)
                right = jnp.where(inside, roll(plane, at - 48 - 64 * field_at, 1), right)
                left = jnp.where(inside, roll(plane, at - 64 * field_at, 1), left)
        rows = slice(16 * group, 16 * group + 16)
        to_first[rows], to_second[rows] = by_side((left, right), odd_z)
    lane = iota((32, 128), 1)
    mirrored = jnp.where((lane & 15) < 8, 7 - (lane & 15), 135 - (lane & 15))
    for local in range(10, 16):
        for part in range(4):
            message[4 * local - 24 + part] = pre[local, 8 * part : 8 * part + 8]
    for group in range(2):
        value = jnp.zeros((32, 128), jnp.float32)
        for slot in range(8):
            inside = (lane >= 16 * slot) & (lane < 16 * slot + 16)
            value = jnp.where(inside, gather_lanes(pre[8 * group + slot], mirrored), value)
        rows = slice(64 - 32 * group, 96 - 32 * group)
        to_first[rows] = value
        to_second[rows] = value


def second_window(place, own, first, second, rhs, coef):
    lane = iota((ROWS, 128), 1)
    odd_y, odd_z = odd_at(place, 1), odd_at(place, 2)

    def page(index):
        low, high = by_side((first[2 * index], second[2 * index]), odd_y)
        low_next, high_next = by_side((first[2 * index + 1], second[2 * index + 1]), odd_y)
        return jnp.concatenate([low, low_next, own[index], high, high_next], axis=0)

    for group in range(4):
        at = (8 + group) if group < 2 else 18 + group
        left, right = by_side((page(at), page(at + 2)), odd_z)
        for slot in range(4):
            other = 4 * group + slot
            local, middle = (other, page(other)) if group < 2 else (23 - other, page(4 + other))
            for field_at, array in enumerate((rhs, coef)):
                at = 32 * slot + 16 * field_at
                value = jnp.where(lane < 64, roll(middle, -64 * field_at, 1), 0.0)
                value = jnp.where((lane >= 64) & (lane < 80), roll(right, 64 - at, 1), value)
                array[block(main_at(local + 1), ROWS)] = jnp.where(lane >= 112, roll(left, 112 - at, 1), value)


def second_sweep(count, kept, source, target, skip=0, keep=1.0 - DAMPING):
    rows = ROWS - 2 * skip
    at = block(main_at(0) + skip, rows)
    flux = kept[0, at] * source[at]
    here = source[block(main_at(1) + skip, rows)]
    for plane in range(1, count + 1):
        at = block(main_at(plane) + skip, rows)
        after = source[block(main_at(plane + 1) + skip, rows)]
        face = kept[0, at]
        total = flux + face * after
        flux = face * here
        total = total + both_ways(kept[1, at], here, 0) + both_ways(kept[2, at], here, 1)
        target[at] = kept[4, at] + keep * here + kept[3, at] * total
        here = after


def second_kernel(own, first, second, share, va, kept, rhs, coef, inverse, vb, sums):
    place = device_place()
    blank = jnp.zeros((ROWS, 128), jnp.float32)
    for plane in (0, 17):
        at = block(main_at(plane), ROWS)
        for array in (coef, va, vb, kept.at[0], kept.at[4]):
            array[at] = blank
    second_window(place, own, first, second, rhs, coef)

    def plane(index):
        at = block(main_at(index + 1), ROWS)
        here = coef[at]
        nears = [coef[block(main_at(index + 2), ROWS)], coef[block(main_at(index), ROWS)],
                 roll(here, -1, 0), roll(here, 1, 0), roll(here, -1, 1), roll(here, 1, 1)]
        faces, scale, start, inverse[at] = terms(here, nears, rhs[at], 0.25)
        for side, value in enumerate((faces[0], faces[2], faces[4], scale, start)):
            kept[side, at] = value

    each(16, plane, 4)
    second_sweep(16, kept, kept.at[4], va)

    def twice(index, carry):
        second_sweep(16, kept, va, vb)
        second_sweep(16, kept, vb, va)
        return carry

    lax.fori_loop(0, 2, twice, 0)
    second_sweep(16, kept, va, vb, 8, -DAMPING)
    for local in range(8):
        residual = jnp.zeros((16, 128), jnp.float32)
        conduct = jnp.zeros((16, 128), jnp.float32)
        for here in (2 * local + 1, 2 * local + 2):
            at = block(main_at(here) + 16, 16)
            residual = residual + vb[at] * inverse[at]
            conduct = conduct + coef[at]
        sums[16 * local : 16 * local + 16] = residual
        sums[128 + 16 * local : 144 + 16 * local] = conduct
    folded = lane_pairs(row_pairs(sums, 256)) * 0.125
    lane = iota((8, 128), 1)
    for group in range(4):
        value = jnp.zeros((8, 128), jnp.float32)
        for plane in range(2):
            for field_at in range(2):
                row = 64 * field_at + 8 * (2 * group + plane)
                at = 64 * plane + 32 * field_at
                inside = (lane >= at) & (lane < at + 32)
                value = jnp.where(inside, gather_lanes(folded[row : row + 8], (2 * lane) & 63), value)
        for device in range(share.shape[0]):
            share[device, group] = value


def whole_terms(planes, rows, lanes, rhs, coef, kept, weight):
    row = iota((rows, 128), 0)
    lane = iota((rows, 128), 1)
    outside = jnp.zeros((rows, 128), jnp.float32)
    held = [outside] + [coef[here] for here in range(planes)] + [outside]
    for here in range(planes):
        middle = held[here + 1]
        nears = [
            held[here + 2], held[here],
            jnp.where(row == rows - 1, 0.0, roll(middle, -1, 0)), jnp.where(row == 0, 0.0, roll(middle, 1, 0)),
            jnp.where(lane >= lanes - 1, 0.0, roll(middle, -1, 1)), jnp.where(lane == 0, 0.0, roll(middle, 1, 1))]
        faces, scale, start, back = terms(middle, nears, rhs[here], weight)
        for side in range(3):
            kept[side, here] = jnp.where(nears[2 * side] > 0.0, faces[2 * side], 0.0)
        kept[3, here] = scale
        kept[4, here] = start
        kept[5, here] = back


def whole_change(kept, values, keep):
    found = []
    flux = None
    for here, value in enumerate(values):
        total = both_ways(kept[1, here], value, 0) + both_ways(kept[2, here], value, 1)
        if here > 0:
            total = total + flux
        if here + 1 < len(values):
            face = kept[0, here]
            total = total + face * values[here + 1]
            flux = face * value
        found.append(kept[4, here] + keep * value + kept[3, here] * total)
    return tuple(found)


def whole_sweeps(count, kept, values):
    return lax.fori_loop(0, count, lambda index, held: whole_change(kept, held, 1.0 - DAMPING), tuple(values))


def whole_solve(level, scratch):
    kept, rhs, coef, rows_of = scratch[0]
    planes, rows = rhs.shape[0], rhs.shape[1]
    lanes = 128 >> (level - 2)
    whole_terms(planes, rows, lanes, rhs, coef, kept, 0.25**level)
    start = [kept[4, here] for here in range(planes)]
    values = whole_sweeps((COARSE_SWEEPS if level == 4 else SWEEPS) - 1, kept, start)
    if level < 4:
        residual = [value * kept[5, here] for here, value in enumerate(whole_change(kept, values, -DAMPING))]
        size = planes // 2 * rows
        for pair in range(planes // 2):
            at = pair * rows
            rows_of[at : at + rows] = residual[2 * pair] + residual[2 * pair + 1]
            rows_of[size + at : size + at + rows] = coef[2 * pair] + coef[2 * pair + 1]
        folded = lane_pairs(row_pairs(rows_of, 2 * size)) * 0.125
        lane = iota(folded.shape, 1)
        folded = jnp.where(lane < lanes // 2, gather_lanes(folded, (2 * lane) & 127), 0.0)
        half = rows // 2
        for pair in range(planes // 2):
            scratch[1][1][pair] = folded[pair * half : pair * half + half]
            scratch[1][2][pair] = folded[size // 2 + pair * half : size // 2 + pair * half + half]
        lower = jnp.concatenate(whole_solve(level + 1, scratch[1:]), axis=0)
        repeat_rows(rows_of.at[0:size], gather_lanes(lower, lax.shift_right_logical(iota(lower.shape, 1), 1)))
        values = [
            value + rows_of[here // 2 * rows : here // 2 * rows + rows] for here, value in enumerate(values)]
        values = whole_sweeps(SWEEPS, kept, values)
    return list(values)


def whole_scratch(planes, rows):
    return [field(6, planes, rows, 128), field(planes, rows, 128), field(planes, rows, 128), field(planes * rows, 128)]


def third_whole(shares, count_y, count_z, rhs, coef):
    lane = iota((8, 128), 1)
    width = 128 // count_z
    for local in range(8):
        for at_y in range(count_y):
            for index, array in enumerate((rhs, coef)):
                value = jnp.zeros((8, 128), jnp.float32)
                for at_z in range(count_z):
                    held = shares[at_y * count_z + at_z, local // 2]
                    at = 64 * (local % 2) + 32 * index
                    inside = (lane >= width * at_z) & (lane < width * at_z + width)
                    value = jnp.where(inside, roll(held, width * at_z - at, 1), value)
                array[local, 8 * at_y : 8 * at_y + 8] = value


def last_kernel(count_y, count_z, own2, first1, second1, shares, pre1, kept1, kept, kept_strip, out, *scratch):
    place = device_place()
    deep = [scratch[0:4], scratch[4:8], scratch[8:12]]
    va1, vb1, va, va_strip, vb, vb_strip = scratch[12:18]
    framed, twice1, twice0 = scratch[18:21]
    third_whole(shares, count_y, count_z, deep[0][1], deep[0][2])
    third = whole_solve(2, deep)

    blank = jnp.zeros((ROWS, 128), jnp.float32)
    for array, outer in ((va1, 17), (va_strip, 4), (vb_strip, 4)):
        array[block(main_at(outer), ROWS)] = blank
    for array in (va1, va, va_strip, vb, vb_strip):
        array[block(main_at(0), ROWS)] = blank
    rows = third[0].shape[0]
    for index, plane in enumerate(third):
        framed[index, 0:8] = blank[0:8]
        framed[index, 8 : 8 + rows] = plane
        framed[index, 8 + rows : 16 + rows] = blank[0:8]
    for index in range(8):
        near = framed[index, pl.ds(pl.multiple_of(8 * place[1], 8), 24), :]
        repeat_rows(twice1.at[48 * index : 48 * index + 48], near)
    lane = iota((ROWS, 128), 1)
    held = lax.shift_right_arithmetic(jnp.where(lane < 96, lane, lane - 128), 1) + 32 * place[2]
    inside = (held >= 0) & (held < 128) & ((lane < 80) | (lane >= 112))
    for index in range(8):
        wide = jnp.where(inside, gather_lanes(twice1[48 * index : 48 * index + 48], held & 127), 0.0)
        for here in (2 * index + 1, 2 * index + 2):
            there = block(main_at(here), ROWS)
            va1[there] = pre1[there] + jnp.where(kept1[3, there] > 0.0, wide, 0.0)
    vb1[block(main_at(0), ROWS)] = blank
    vb1[block(main_at(17), ROWS)] = blank
    source, target = va1, vb1
    for sweep in range(SWEEPS):
        second_sweep(16 - sweep, kept1, source, target, 8 if sweep else 0)
        source, target = target, source

    odd_y = odd_at(place, 1)

    def page(index):
        low, high = by_side((first1[48 + index], second1[48 + index]), odd_y)
        return jnp.concatenate([low, own2[index], high], axis=0)

    slot_lane = lane & 15
    above = slot_lane < 8
    facing_lane = jnp.where(above, 64 + lax.shift_right_logical(7 - slot_lane, 1), 127 - lax.shift_right_logical(slot_lane - 8, 1))
    for group in range(3):
        more = jnp.zeros((ROWS, 128), jnp.float32)
        for index in range(4 * group, min(4 * group + 4, 11)):
            at = main_at(index + 1) + 8
            repeat_rows(twice0, source[at : at + 32])
            near = twice0[8:56]
            wide = gather_lanes(near, lax.shift_right_logical(lane, 1))
            at = 32 * (index - 4 * group)
            more = jnp.where((lane >= at) & (lane < at + 32), gather_lanes(near, facing_lane & 127), more)
            for local in (2 * index, 2 * index + 1):
                there = block(main_at(local + 1), ROWS)
                middle = page(local if local < 16 else 39 - local)
                va[there] = middle + jnp.where(kept[4, there] > 0.0, wide, 0.0)
        value = mirrored_slots(page(24)) if group == 2 else page(17 - group)
        there = block(main_at(group + 1), ROWS)
        va_strip[there] = value + jnp.where(kept_strip[0, there] > 0.0, more, 0.0)
    source, target = (va, va_strip), (vb, vb_strip)
    for count in range(21, 15, -1):
        finest_sweep(count, (kept, kept_strip), source, target, strips=count > 16)
        source, target = target, source

    def leave(local):
        out[local + place[0] * (15 - 2 * local)] = source[0][block(main_at(local + 1) + 8, 32)]

    each(16, leave, 4)


def call(kernel, inputs, outs, scratch):
    near = pl.BlockSpec(memory_space=pltpu.VMEM)
    return pl.pallas_call(
        kernel,
        out_shape=[jax.ShapeDtypeStruct(shape, jnp.float32) for shape in outs],
        in_specs=[near] * len(inputs),
        out_specs=[near] * len(outs),
        scratch_shapes=scratch,
        compiler_params=pltpu.CompilerParams(vmem_limit_bytes=VMEM_BYTES),
    )(*inputs)


def field(*shape):
    return pltpu.VMEM(shape, jnp.float32)


def from_sides(axis, to_first, to_second):
    size = lax.axis_size(axis)
    found = []
    for message, begin in ((to_second, 1), (to_first, 0)):
        lower = [(i, i + 1) for i in range(begin, size - 1, 2)]
        found.append(lax.ppermute(message, axis, lower + [(j, i) for i, j in lower]))
    return found[::-1]


def edge_rows(array, axis, last):
    odd = lax.axis_index(axis) % 2
    rows = array.shape[1]
    return lax.dynamic_slice_in_dim(array, (rows - 8) * (odd if last else 1 - odd), 8, 1)


def from_partner(message):
    return lax.ppermute(message, "gx", [(0, 1), (1, 0)])


def merged_sides(first, second):
    odd = lax.axis_index("gz") % 2 == 1
    above = lax.broadcasted_iota(jnp.int32, first.shape, first.ndim - 1) % 16 < 8
    return jnp.where(above == odd, second, first)


def fast_shards(source, conductivity):
    count_y, count_z = lax.axis_size("gy"), lax.axis_size("gz")
    own, message = call(plane_kernel, (source, conductivity), [(32, 32, 128), (13, 32, 128)], [])
    to_first, to_second, *rows = call(
        edge_kernel, (own,), [(2, 32, 128), (2, 32, 128), (32, 8, 128), (32, 8, 128)], [])
    partner = from_partner(message)
    strips = jnp.concatenate(from_sides("gz", to_first, to_second)[::-1])
    own_rev = from_sides("gy", *rows)[::-1]
    own_rev = lax.optimization_barrier(own_rev)
    own_rows = own_rev[::-1]
    strip_rows = from_sides("gy", *(edge_rows(strips, "gy", last) for last in (False, True)))
    message = jnp.concatenate(
        [strips[1].reshape(4, 8, 128), strips[3].reshape(4, 8, 128)]
        + [part for array in own_rows for part in (array[11:16], array[26:32])])
    beside = from_partner(message)
    strip_rows, _ = lax.optimization_barrier((strip_rows, message))
    corner = from_partner(jnp.concatenate([array[at : at + 1] for array in strip_rows for at in (1, 3)]))

    main, strip = field(MAIN, 128), field(STRIP, 128)
    kept = [(6, MAIN, 128), (7, STRIP, 128)]
    pre, lower, message, to_first, to_second, *kept0 = call(
        finest_kernel,
        (own, strips, *own_rows, *strip_rows, partner, beside, corner),
        [(16, 32, 128), (8, 16, 128), (40, 8, 128), (96, 128), (96, 128), *kept],
        [main, strip] * 4 + [main, field(512, 128)])
    partner = from_partner(message)
    strips = from_sides("gz", to_first, to_second)
    lower_strips = jnp.concatenate([part[:32].reshape(4, 8, 128) for part in strips])
    pre_strips = merged_sides(*(part[32:].reshape(2, 32, 128) for part in strips))
    further = from_partner(jnp.concatenate([lower_strips, pre_strips[0].reshape(4, 8, 128)]))
    flat = jnp.concatenate([lower.reshape(16, 8, 128), lower_strips, partner[:16], further[:8]])
    own2 = jnp.concatenate([pre, pre_strips, partner[16:].reshape(6, 32, 128), further[8:].reshape(1, 32, 128)])
    rows1 = from_sides("gy", *(jnp.concatenate([flat, edge_rows(own2, "gy", last)]) for last in (False, True)))

    window = field(SECOND, 128)
    share, *kept1 = call(
        second_kernel,
        (flat.reshape(24, 16, 128), *rows1),
        [(count_y * count_z, 4, 8, 128), (SECOND, 128), (5, SECOND, 128)],
        [window] * 4 + [field(256, 128)])
    shares = lax.all_to_all(share, ("gy", "gz"), 0, 0, tiled=True)

    scratch = whole_scratch(8, 32) + whole_scratch(4, 16) + whole_scratch(2, 8)
    scratch += [window, window] + [main, strip] * 2 + [field(8, 48, 128), field(384, 128), field(64, 128)]
    (result,) = call(
        functools.partial(last_kernel, count_y, count_z),
        (own2, *rows1, shares, *kept1, *kept0),
        [(16, 32, 128)],
        scratch)
    return result


def solution(mesh):
    in_specs = (P("gx", "gy", "gz"), P("gx", "gy", "gz"))
    out_specs = P("gx", "gy", "gz")

    def run(source, conductivity):
        counts = tuple(mesh.shape[axis] for axis in ("gx", "gy", "gz"))
        held = tuple(size // count for size, count in zip(source.shape, counts))
        fast = counts == (2, 4, 4) and held == (16, 32, 128)
        shards = fast_shards if fast else plain_shards
        return jax.shard_map(shards, mesh=mesh, in_specs=in_specs, out_specs=out_specs, check_vma=False)(source, conductivity)

    return run
```

```python
import functools

import jax
import jax.numpy as jnp
from jax import lax
from jax.experimental import pallas as pl
from jax.experimental.pallas import tpu as pltpu
from jax.sharding import PartitionSpec as P

SWEEPS = 6
COARSE_SWEEPS = 16
DAMPING = 0.8
VMEM_BYTES = 32 * 2**20


def with_halo(array, sides, width):
    for axis, dim in sides:
        size, length = (lax.axis_size(axis), array.shape[dim])
        up = [(i, (i + 1) % size) for i in range(size - 1)]
        down = [(j, i) for i, j in up]
        last = lax.slice_in_dim(array, length - width, length, axis=dim)
        first = lax.slice_in_dim(array, 0, width, axis=dim)
        before = lax.ppermute(last, axis, up)
        after = lax.ppermute(first, axis, down)
        array = jnp.concatenate([before, array, after], axis=dim)
    return array


def centre(padded):
    return padded[1:-1, 1:-1, 1:-1]


def neighbours(padded):
    return [
        padded[2:, 1:-1, 1:-1],
        padded[:-2, 1:-1, 1:-1],
        padded[1:-1, 2:, 1:-1],
        padded[1:-1, :-2, 1:-1],
        padded[1:-1, 1:-1, 2:],
        padded[1:-1, 1:-1, :-2],
    ]


def zero_pad(field):
    return jnp.pad(field, 1)


def stencil(field_pad, coef_pad, weight):
    middle = centre(field_pad)
    coef_mid = centre(coef_pad)
    total = jnp.zeros_like(middle)
    for field_near, coef_near in zip(neighbours(field_pad), neighbours(coef_pad)):
        total = total + 0.5 * (coef_mid + coef_near) * (middle - field_near)
    return weight * total


def diagonal(coef_pad, weight):
    coef_mid = centre(coef_pad)
    total = jnp.zeros_like(coef_mid)
    for coef_near in neighbours(coef_pad):
        total = total + 0.5 * (coef_mid + coef_near)
    return weight * total


def restrict(field):
    shape = field.shape
    blocks = field.reshape(shape[0] // 2, 2, shape[1] // 2, 2, shape[2] // 2, 2)
    return blocks.mean(axis=(1, 3, 5))


def prolong(field):
    return jnp.repeat(jnp.repeat(jnp.repeat(field, 2, 0), 2, 1), 2, 2)


def jacobi(field, rhs_level, coef_pad, diag_terms, weight, padder):
    return field + DAMPING * (rhs_level - stencil(padder(field), coef_pad, weight)) / diag_terms


def face_rim(field):
    return with_halo(field, (("gx", 0), ("gy", 1), ("gz", 2)), 1)


def slab_pad(field):
    extended = with_halo(field, (("gx", 0),), 1)
    return jnp.pad(extended, ((0, 0), (1, 1), (1, 1)))


def single_sweeps(field, rhs_level, coef_pad, diag_terms, weight):
    for sweep_index in range(SWEEPS):
        field = jacobi(field, rhs_level, coef_pad, diag_terms, weight, face_rim)
    return field


def coarse_solve(rhs_level, coef_level):
    weight = 0.25**4
    coef_pad = zero_pad(coef_level)
    diag_terms = diagonal(coef_pad, weight)

    def coarse_step(count, field):
        return jacobi(field, rhs_level, coef_pad, diag_terms, weight, zero_pad)

    return lax.fori_loop(0, COARSE_SWEEPS, coarse_step, jnp.zeros_like(rhs_level))


def level_three(rhs_level, coef_level, padder, lower_solve):
    weight = 0.25**3
    coef_pad = padder(coef_level)
    diag_terms = diagonal(coef_pad, weight)
    field = jnp.zeros_like(rhs_level)
    for sweep_index in range(SWEEPS):
        field = jacobi(field, rhs_level, coef_pad, diag_terms, weight, padder)
    residual = rhs_level - stencil(padder(field), coef_pad, weight)
    field = field + prolong(lower_solve(restrict(residual), restrict(coef_level)))
    for sweep_index in range(SWEEPS):
        field = jacobi(field, rhs_level, coef_pad, diag_terms, weight, padder)
    return field


def plain_shards(source, conductivity):
    count_x, count_y, count_z = (lax.axis_size("gx"), lax.axis_size("gy"), lax.axis_size("gz"))
    place_x, place_y, place_z = (lax.axis_index("gx"), lax.axis_index("gy"), lax.axis_index("gz"))
    rhs_level = source
    coef_level = conductivity
    saved = []
    for level_index in range(3):
        weight = 0.25**level_index
        coef_pad = face_rim(coef_level)
        diag_terms = diagonal(coef_pad, weight)
        extras = None
        field = single_sweeps(jnp.zeros_like(rhs_level), rhs_level, coef_pad, diag_terms, weight)
        residual = rhs_level - stencil(face_rim(field), coef_pad, weight)
        saved.append((field, rhs_level, coef_pad, diag_terms, weight, extras))
        rhs_level = restrict(residual)
        coef_level = restrict(coef_level)
    rows_x, rows_y, rows_z = rhs_level.shape
    stacked = jnp.stack([rhs_level, coef_level])[None]
    gathered = lax.all_gather(stacked, ("gy", "gz"), axis=0, tiled=True)
    slab = gathered.reshape(count_y, count_z, 2, rows_x, rows_y, rows_z)
    slab = slab.transpose(2, 3, 0, 4, 1, 5).reshape(2, rows_x, count_y * rows_y, count_z * rows_z)

    def lower_groups(rhs_low, coef_low):
        lowered = lax.all_gather(jnp.stack([rhs_low, coef_low]), "gx", axis=1, tiled=True)
        whole = coarse_solve(lowered[0], lowered[1])
        return lax.dynamic_slice_in_dim(whole, place_x * (rows_x // 2), rows_x // 2, 0)

    field = level_three(slab[0], slab[1], slab_pad, lower_groups)
    field = lax.dynamic_slice_in_dim(field, place_y * rows_y, rows_y, 1)
    result = lax.dynamic_slice_in_dim(field, place_z * rows_z, rows_z, 2)
    for level_index in (2, 1, 0):
        field, rhs_here, coef_pad, diag_terms, weight, extras = saved[level_index]
        field = field + prolong(result)
        field = single_sweeps(field, rhs_here, coef_pad, diag_terms, weight)
        result = field
    return result


ROWS = 48
MARGIN = 8
MAIN = MARGIN + 25 * ROWS + MARGIN
STRIP = MARGIN + 5 * ROWS + MARGIN
SECOND = MARGIN + 18 * ROWS + MARGIN


def roll(value, shift, axis):
    if isinstance(shift, int):
        shift = shift % value.shape[axis]
        if shift == 0:
            return value
    return pltpu.roll(value, shift, axis)


def iota(shape, axis):
    return lax.broadcasted_iota(jnp.int32, shape, axis)


def gather_lanes(value, lanes):
    return jnp.take_along_axis(value, lanes, axis=1, mode="promise_in_bounds")


def block(at, count):
    return pl.ds(pl.multiple_of(at, 8) if not isinstance(at, int) else at, count)


def terms(coef, nears, rhs, weight):
    faces = [0.5 * (coef + near) for near in nears]
    total = functools.reduce(lambda a, b: a + b, faces)
    scale = jnp.where(coef > 0.0, DAMPING / total, 0.0)
    return faces, scale, rhs * scale * (1.0 / weight), total * (weight / DAMPING)


def each(count, body, step):
    def several(turn, carry):
        for ahead in range(step):
            body(turn * step + ahead)
        return carry

    def single(index, carry):
        body(index)
        return carry

    whole = count // step
    lax.fori_loop(0, whole, several, 0)
    if count % step:
        lax.fori_loop(whole * step, count, single, 0)


def row_pairs(array, rows):
    return array[pl.ds(0, rows // 2, stride=2), :] + array[pl.ds(1, rows // 2, stride=2), :]


def repeat_rows(array, value):
    rows = value.shape[0]
    array[pl.ds(0, rows, stride=2), :] = value
    array[pl.ds(1, rows, stride=2), :] = value


def lane_pairs(value):
    return value + roll(value, -1, 1)


def both_ways(face, value, axis):
    return face * roll(value, -1, axis) + roll(face * value, 1, axis)


def by_side(swapped, odd):
    first, second = swapped
    return jnp.where(odd, first, second), jnp.where(odd, second, first)


def device_place():
    return [lax.axis_index(axis) for axis in ("gx", "gy", "gz")]


def odd_at(place, axis):
    return (place[axis] & 1) == 1


def with_tiles(middle, first, second, odd):
    sides = [by_side(tiles, odd) for tiles in zip(first, second)]
    return jnp.concatenate([low for low, _ in sides] + list(middle) + [high for _, high in sides], axis=0)


def main_at(plane):
    return MARGIN + ROWS * plane


def joined(middle, edge):
    lane = iota(middle.shape, 1)
    return jnp.where(lane == 127, edge, roll(middle, -1, 1)), jnp.where(lane == 0, edge, roll(middle, 1, 1))


def facing(own, plane, slot):
    lane = iota(own.shape, 1)
    return jnp.where((lane == 16 * slot + 7) | (lane == 16 * slot + 8), roll(plane, 16 * slot + 8, 1), own)


def strip_nears(strip, own, group):
    at = main_at(group + 1)
    middle = strip[block(at, ROWS)]
    lane = iota((ROWS, 128), 1)
    slot_lane = lane & 15
    further = jnp.where(lane < 112, roll(middle, -16, 1), roll(strip[block(at + ROWS, ROWS)], -16, 1))
    nearer = jnp.where(lane >= 16, roll(middle, 16, 1), roll(strip[block(at - ROWS, ROWS)], 16, 1))
    after = jnp.where(slot_lane == 7, own, roll(middle, -1, 1))
    before = jnp.where(slot_lane == 8, own, roll(middle, 1, 1))
    return middle, [further, nearer, roll(middle, -1, 0), roll(middle, 1, 0), after, before]


def finest_terms(rhs, coef, kept, inverse):
    main, strip = coef

    def group(index, slots):
        first = 8 * index + 1
        before = main[block(main_at(first - 1), ROWS)]
        here = main[block(main_at(first), ROWS)]
        held = strip[block(main_at(index + 1), ROWS)]
        own = jnp.zeros((ROWS, 128), jnp.float32)
        for slot in range(slots):
            at = block(main_at(first + slot), ROWS)
            after = main[block(main_at(first + slot + 1), ROWS)]
            nears = [after, before, roll(here, -1, 0), roll(here, 1, 0), *joined(here, roll(held, 120 - 16 * slot, 1))]
            faces, scale, start, back = terms(here, nears, rhs[0][at], 1.0)
            for side, value in enumerate((faces[0], faces[2], faces[4], faces[5], scale, start)):
                kept[0][side, at] = value
            inverse[at] = back
            own = facing(own, here, slot)
            before, here = here, after
        for slot in range(slots, 8):
            own = facing(own, main[block(main_at(first + slot), ROWS)], slot)
        at = block(main_at(index + 1), ROWS)
        middle, nears = strip_nears(strip, own, index)
        faces, scale, start, _ = terms(middle, nears, rhs[1][at], 1.0)
        for side in range(6):
            kept[1][side, at] = faces[side] * scale
        kept[1][6, at] = start

    each(2, lambda index: group(index, 8), 1)
    group(2, 6)


def finest_sweep(count, kept, source, target, keep=1.0 - DAMPING, strips=True):
    main, strip = source

    def group(index, slots):
        first = 8 * index + 1
        at = block(main_at(first - 1), ROWS)
        flux = kept[0][0, at] * main[at]
        here = main[block(main_at(first), ROWS)]
        held = strip[block(main_at(index + 1), ROWS)]
        own = jnp.zeros((ROWS, 128), jnp.float32)
        for slot in range(slots):
            at = block(main_at(first + slot), ROWS)
            after = main[block(main_at(first + slot + 1), ROWS)]
            face = kept[0][0, at]
            total = flux + face * after
            flux = face * here
            total = total + both_ways(kept[0][1, at], here, 0)
            above, below = joined(here, roll(held, 120 - 16 * slot, 1))
            total = total + kept[0][2, at] * above + kept[0][3, at] * below
            target[0][at] = kept[0][5, at] + keep * here + kept[0][4, at] * total
            if strips:
                own = facing(own, here, slot)
            here = after
        if strips:
            at = block(main_at(index + 1), ROWS)
            middle, nears = strip_nears(strip, own, index)
            total = kept[1][6, at] + keep * middle
            for side, near in enumerate(nears):
                total = total + kept[1][side, at] * near
            target[1][at] = total

    each(2, lambda index: group(index, 8), 1)
    if count > 16:
        group(2, count - 16)


def strip_pages(rhs_planes, coef_planes):
    lane = iota((32, 128), 1)
    left = jnp.zeros((32, 128), jnp.float32)
    right = jnp.zeros((32, 128), jnp.float32)
    for field_at, planes in ((0, rhs_planes), (8, coef_planes)):
        for slot, plane in enumerate(planes):
            at = 16 * slot + field_at
            inside = (lane >= at) & (lane < at + 8)
            left = jnp.where(inside, gather_lanes(plane, 7 - (lane & 7)), left)
            right = jnp.where(inside, gather_lanes(plane, 127 - (lane & 7)), right)
    return left, right


def pack_kernel(own, message, to_first, to_second, rows_first, rows_second):
    place = device_place()
    odd, odd_y = odd_at(place, 2), odd_at(place, 1)
    for group in range(2):
        planes = ([], [])
        for local in range(8 * group, 8 * group + 8):
            held = local + place[0] * (15 - 2 * local)
            for field_at in range(2):
                plane = own[16 * field_at + held]
                at = 16 * field_at + local
                rows_first[at], rows_second[at] = by_side((plane[0:8], plane[24:32]), odd_y)
                if local > 9 - field_at:
                    message[6 * field_at + 15 - local] = plane
                planes[field_at].append(plane)
        to_first[group], to_second[group] = by_side(strip_pages(*planes), odd)


def mirrored_slots(value):
    lane = iota(value.shape, 1)
    found = value
    for slot in range(8):
        inside = (lane >= 16 * slot) & (lane < 16 * slot + 16)
        found = jnp.where(inside, roll(value, 16 * (2 * slot - 7), 1), found)
    return found


def finest_kernel(own, strips, own_first, own_second, strip_first, strip_second, partner, beside, corner, pre, lower, message,
                  to_first, to_second, kept, kept_strip, rhs, rhs_strip, coef, coef_strip, va, va_strip, vb, vb_strip, inverse,
                  sums):
    place = device_place()
    blank = jnp.zeros((ROWS, 128), jnp.float32)
    outside = block(main_at(0), ROWS)
    for array in (coef, va, vb):
        array[outside] = blank
    coef[block(main_at(24), ROWS)] = blank
    kept[0, outside] = blank
    kept[5, outside] = blank
    for array in (coef_strip, va_strip, vb_strip, kept_strip.at[6]):
        array[outside] = blank
        array[block(main_at(4), ROWS)] = blank
    odd_y, odd_z = odd_at(place, 1), odd_at(place, 2)

    for local in range(23):
        at = block(main_at(local + 1), ROWS)
        for field_at, array in enumerate((rhs, coef)):
            if local < 16:
                page = 16 * field_at + local
                held = 16 * field_at + local + place[0] * (15 - 2 * local)
                array[at] = with_tiles([own[held]], [own_first[page]], [own_second[page]], odd_y)
            elif local < 22 + field_at:
                step = local - 16
                page = 13 + 7 * field_at - step
                array[at] = with_tiles([partner[6 * field_at + step]], [beside[page]], [beside[13 + page]], odd_y)
    above = (iota((ROWS, 128), 1) & 15) < 8
    for group in range(3):
        pages = []
        for which in range(2):
            if group < 2:
                page = 2 - 2 * which + group
                pages.append(with_tiles([strips[page]], [strip_first[page]], [strip_second[page]], odd_y))
            else:
                tiles = [beside[4 - 4 * which + part] for part in range(4)]
                pages.append(with_tiles(tiles, [corner[1 - which]], [corner[3 - which]], odd_y))
        left, right = by_side(pages, odd_z)
        if group == 2:
            left, right = mirrored_slots(left), mirrored_slots(right)
        at = block(main_at(group + 1), ROWS)
        rhs_strip[at] = jnp.where(above, right, roll(left, 8, 1))
        coef_strip[at] = jnp.where(above, roll(right, -8, 1), left)
    both = (kept, kept_strip)
    finest_terms((rhs, rhs_strip), (coef, coef_strip), both, inverse)
    a, b = (va, va_strip), (vb, vb_strip)
    source = (kept.at[5], kept_strip.at[6])
    for count, target in zip(range(21, 16, -1), (a, b, a, b, a)):
        finest_sweep(count, both, source, target)
        source = target
    finest_sweep(16, both, a, b, -DAMPING, False)

    def pair(index):
        total = jnp.zeros((32, 128), jnp.float32)
        conduct = jnp.zeros((32, 128), jnp.float32)
        for local in (2 * index, 2 * index + 1):
            at = block(main_at(local + 1) + 8, 32)
            value = va[at]
            pre[local] = value
            total = total + vb[at] * inverse[at]
            conduct = conduct + coef[at]
        sums[block(index * 32, 32)] = total
        sums[block(index * 32 + 256, 32)] = conduct

    each(8, pair, 4)
    folded = lane_pairs(row_pairs(sums, 512)) * 0.125
    lane = iota((128, 128), 1)
    merged = jnp.where(lane < 64, gather_lanes(folded[0:128], (2 * lane) & 127), gather_lanes(folded[128:256], (2 * lane) & 127))
    lane = iota((16, 128), 1)
    for group in range(2):
        right = jnp.zeros((16, 128), jnp.float32)
        left = jnp.zeros((16, 128), jnp.float32)
        for slot in range(4):
            local = 4 * group + slot
            plane = merged[16 * local : 16 * local + 16]
            lower[local] = plane
            message[2 * local] = plane[0:8]
            message[2 * local + 1] = plane[8:16]
            for field_at in range(2):
                at = 32 * slot + 16 * field_at
                inside = (lane >= at) & (lane < at + 16)
                right = jnp.where(inside, roll(plane, at - 48 - 64 * field_at, 1), right)
                left = jnp.where(inside, roll(plane, at - 64 * field_at, 1), left)
        rows = slice(16 * group, 16 * group + 16)
        to_first[rows], to_second[rows] = by_side((left, right), odd_z)
    lane = iota((32, 128), 1)
    mirrored = jnp.where((lane & 15) < 8, 7 - (lane & 15), 135 - (lane & 15))
    for local in range(10, 16):
        for part in range(4):
            message[4 * local - 24 + part] = pre[local, 8 * part : 8 * part + 8]
    for group in range(2):
        value = jnp.zeros((32, 128), jnp.float32)
        for slot in range(8):
            inside = (lane >= 16 * slot) & (lane < 16 * slot + 16)
            value = jnp.where(inside, gather_lanes(pre[8 * group + slot], mirrored), value)
        rows = slice(64 - 32 * group, 96 - 32 * group)
        to_first[rows] = value
        to_second[rows] = value


def second_window(place, own, first, second, rhs, coef):
    lane = iota((ROWS, 128), 1)
    odd_y, odd_z = odd_at(place, 1), odd_at(place, 2)

    def page(index):
        low, high = by_side((first[2 * index], second[2 * index]), odd_y)
        low_next, high_next = by_side((first[2 * index + 1], second[2 * index + 1]), odd_y)
        return jnp.concatenate([low, low_next, own[index], high, high_next], axis=0)

    for group in range(4):
        at = (8 + group) if group < 2 else 18 + group
        left, right = by_side((page(at), page(at + 2)), odd_z)
        for slot in range(4):
            other = 4 * group + slot
            local, middle = (other, page(other)) if group < 2 else (23 - other, page(4 + other))
            for field_at, array in enumerate((rhs, coef)):
                at = 32 * slot + 16 * field_at
                value = jnp.where(lane < 64, roll(middle, -64 * field_at, 1), 0.0)
                value = jnp.where((lane >= 64) & (lane < 80), roll(right, 64 - at, 1), value)
                array[block(main_at(local + 1), ROWS)] = jnp.where(lane >= 112, roll(left, 112 - at, 1), value)


def second_sweep(count, kept, source, target, skip=0, keep=1.0 - DAMPING):
    rows = ROWS - 2 * skip
    at = block(main_at(0) + skip, rows)
    flux = kept[0, at] * source[at]
    here = source[block(main_at(1) + skip, rows)]
    for plane in range(1, count + 1):
        at = block(main_at(plane) + skip, rows)
        after = source[block(main_at(plane + 1) + skip, rows)]
        face = kept[0, at]
        total = flux + face * after
        flux = face * here
        total = total + both_ways(kept[1, at], here, 0) + both_ways(kept[2, at], here, 1)
        target[at] = kept[4, at] + keep * here + kept[3, at] * total
        here = after


def second_kernel(own, first, second, share, va, kept, rhs, coef, inverse, vb, sums):
    place = device_place()
    blank = jnp.zeros((ROWS, 128), jnp.float32)
    for plane in (0, 17):
        at = block(main_at(plane), ROWS)
        for array in (coef, va, vb, kept.at[0], kept.at[4]):
            array[at] = blank
    second_window(place, own, first, second, rhs, coef)

    def plane(index):
        at = block(main_at(index + 1), ROWS)
        here = coef[at]
        nears = [coef[block(main_at(index + 2), ROWS)], coef[block(main_at(index), ROWS)],
                 roll(here, -1, 0), roll(here, 1, 0), roll(here, -1, 1), roll(here, 1, 1)]
        faces, scale, start, inverse[at] = terms(here, nears, rhs[at], 0.25)
        for side, value in enumerate((faces[0], faces[2], faces[4], scale, start)):
            kept[side, at] = value

    each(16, plane, 4)
    second_sweep(16, kept, kept.at[4], va)

    def twice(index, carry):
        second_sweep(16, kept, va, vb)
        second_sweep(16, kept, vb, va)
        return carry

    lax.fori_loop(0, 2, twice, 0)
    second_sweep(16, kept, va, vb, 8, -DAMPING)
    for local in range(8):
        residual = jnp.zeros((16, 128), jnp.float32)
        conduct = jnp.zeros((16, 128), jnp.float32)
        for here in (2 * local + 1, 2 * local + 2):
            at = block(main_at(here) + 16, 16)
            residual = residual + vb[at] * inverse[at]
            conduct = conduct + coef[at]
        sums[16 * local : 16 * local + 16] = residual
        sums[128 + 16 * local : 144 + 16 * local] = conduct
    folded = lane_pairs(row_pairs(sums, 256)) * 0.125
    lane = iota((8, 128), 1)
    for group in range(4):
        value = jnp.zeros((8, 128), jnp.float32)
        for plane in range(2):
            for field_at in range(2):
                row = 64 * field_at + 8 * (2 * group + plane)
                at = 64 * plane + 32 * field_at
                inside = (lane >= at) & (lane < at + 32)
                value = jnp.where(inside, gather_lanes(folded[row : row + 8], (2 * lane) & 63), value)
        for device in range(share.shape[0]):
            share[device, group] = value


def whole_terms(planes, rows, lanes, rhs, coef, kept, weight):
    row = iota((rows, 128), 0)
    lane = iota((rows, 128), 1)
    outside = jnp.zeros((rows, 128), jnp.float32)
    held = [outside] + [coef[here] for here in range(planes)] + [outside]
    for here in range(planes):
        middle = held[here + 1]
        nears = [
            held[here + 2], held[here],
            jnp.where(row == rows - 1, 0.0, roll(middle, -1, 0)), jnp.where(row == 0, 0.0, roll(middle, 1, 0)),
            jnp.where(lane >= lanes - 1, 0.0, roll(middle, -1, 1)), jnp.where(lane == 0, 0.0, roll(middle, 1, 1))]
        faces, scale, start, back = terms(middle, nears, rhs[here], weight)
        for side in range(3):
            kept[side, here] = jnp.where(nears[2 * side] > 0.0, faces[2 * side], 0.0)
        kept[3, here] = scale
        kept[4, here] = start
        kept[5, here] = back


def whole_change(kept, values, keep):
    found = []
    flux = None
    for here, value in enumerate(values):
        total = both_ways(kept[1, here], value, 0) + both_ways(kept[2, here], value, 1)
        if here > 0:
            total = total + flux
        if here + 1 < len(values):
            face = kept[0, here]
            total = total + face * values[here + 1]
            flux = face * value
        found.append(kept[4, here] + keep * value + kept[3, here] * total)
    return tuple(found)


def whole_sweeps(count, kept, values):
    return lax.fori_loop(0, count, lambda index, held: whole_change(kept, held, 1.0 - DAMPING), tuple(values))


def whole_solve(level, scratch):
    kept, rhs, coef, rows_of = scratch[0]
    planes, rows = rhs.shape[0], rhs.shape[1]
    lanes = 128 >> (level - 2)
    whole_terms(planes, rows, lanes, rhs, coef, kept, 0.25**level)
    start = [kept[4, here] for here in range(planes)]
    values = whole_sweeps((COARSE_SWEEPS if level == 4 else SWEEPS) - 1, kept, start)
    if level < 4:
        residual = [value * kept[5, here] for here, value in enumerate(whole_change(kept, values, -DAMPING))]
        size = planes // 2 * rows
        for pair in range(planes // 2):
            at = pair * rows
            rows_of[at : at + rows] = residual[2 * pair] + residual[2 * pair + 1]
            rows_of[size + at : size + at + rows] = coef[2 * pair] + coef[2 * pair + 1]
        folded = lane_pairs(row_pairs(rows_of, 2 * size)) * 0.125
        lane = iota(folded.shape, 1)
        folded = jnp.where(lane < lanes // 2, gather_lanes(folded, (2 * lane) & 127), 0.0)
        half = rows // 2
        for pair in range(planes // 2):
            scratch[1][1][pair] = folded[pair * half : pair * half + half]
            scratch[1][2][pair] = folded[size // 2 + pair * half : size // 2 + pair * half + half]
        lower = jnp.concatenate(whole_solve(level + 1, scratch[1:]), axis=0)
        repeat_rows(rows_of.at[0:size], gather_lanes(lower, lax.shift_right_logical(iota(lower.shape, 1), 1)))
        values = [
            value + rows_of[here // 2 * rows : here // 2 * rows + rows] for here, value in enumerate(values)]
        values = whole_sweeps(SWEEPS, kept, values)
    return list(values)


def whole_scratch(planes, rows):
    return [field(6, planes, rows, 128), field(planes, rows, 128), field(planes, rows, 128), field(planes * rows, 128)]


def third_whole(shares, count_y, count_z, rhs, coef):
    lane = iota((8, 128), 1)
    width = 128 // count_z
    for local in range(8):
        for at_y in range(count_y):
            for index, array in enumerate((rhs, coef)):
                value = jnp.zeros((8, 128), jnp.float32)
                for at_z in range(count_z):
                    held = shares[at_y * count_z + at_z, local // 2]
                    at = 64 * (local % 2) + 32 * index
                    inside = (lane >= width * at_z) & (lane < width * at_z + width)
                    value = jnp.where(inside, roll(held, width * at_z - at, 1), value)
                array[local, 8 * at_y : 8 * at_y + 8] = value


def last_kernel(count_y, count_z, own2, first1, second1, shares, pre1, kept1, kept, kept_strip, out, *scratch):
    place = device_place()
    deep = [scratch[0:4], scratch[4:8], scratch[8:12]]
    va1, vb1, va, va_strip, vb, vb_strip = scratch[12:18]
    framed, twice1, twice0 = scratch[18:21]
    third_whole(shares, count_y, count_z, deep[0][1], deep[0][2])
    third = whole_solve(2, deep)

    blank = jnp.zeros((ROWS, 128), jnp.float32)
    for array, outer in ((va1, 17), (va_strip, 4), (vb_strip, 4)):
        array[block(main_at(outer), ROWS)] = blank
    for array in (va1, va, va_strip, vb, vb_strip):
        array[block(main_at(0), ROWS)] = blank
    rows = third[0].shape[0]
    for index, plane in enumerate(third):
        framed[index, 0:8] = blank[0:8]
        framed[index, 8 : 8 + rows] = plane
        framed[index, 8 + rows : 16 + rows] = blank[0:8]
    for index in range(8):
        near = framed[index, pl.ds(pl.multiple_of(8 * place[1], 8), 24), :]
        repeat_rows(twice1.at[48 * index : 48 * index + 48], near)
    lane = iota((ROWS, 128), 1)
    held = lax.shift_right_arithmetic(jnp.where(lane < 96, lane, lane - 128), 1) + 32 * place[2]
    inside = (held >= 0) & (held < 128) & ((lane < 80) | (lane >= 112))
    for index in range(8):
        wide = jnp.where(inside, gather_lanes(twice1[48 * index : 48 * index + 48], held & 127), 0.0)
        for here in (2 * index + 1, 2 * index + 2):
            there = block(main_at(here), ROWS)
            va1[there] = pre1[there] + jnp.where(kept1[3, there] > 0.0, wide, 0.0)
    vb1[block(main_at(0), ROWS)] = blank
    vb1[block(main_at(17), ROWS)] = blank
    source, target = va1, vb1
    for sweep in range(SWEEPS):
        second_sweep(16 - sweep, kept1, source, target, 8 if sweep else 0)
        source, target = target, source

    odd_y = odd_at(place, 1)

    def page(index):
        low, high = by_side((first1[48 + index], second1[48 + index]), odd_y)
        return jnp.concatenate([low, own2[index], high], axis=0)

    slot_lane = lane & 15
    above = slot_lane < 8
    facing_lane = jnp.where(above, 64 + lax.shift_right_logical(7 - slot_lane, 1), 127 - lax.shift_right_logical(slot_lane - 8, 1))
    for group in range(3):
        more = jnp.zeros((ROWS, 128), jnp.float32)
        for index in range(4 * group, min(4 * group + 4, 11)):
            at = main_at(index + 1) + 8
            repeat_rows(twice0, source[at : at + 32])
            near = twice0[8:56]
            wide = gather_lanes(near, lax.shift_right_logical(lane, 1))
            at = 32 * (index - 4 * group)
            more = jnp.where((lane >= at) & (lane < at + 32), gather_lanes(near, facing_lane & 127), more)
            for local in (2 * index, 2 * index + 1):
                there = block(main_at(local + 1), ROWS)
                middle = page(local if local < 16 else 39 - local)
                va[there] = middle + jnp.where(kept[4, there] > 0.0, wide, 0.0)
        value = mirrored_slots(page(24)) if group == 2 else page(17 - group)
        there = block(main_at(group + 1), ROWS)
        va_strip[there] = value + jnp.where(kept_strip[0, there] > 0.0, more, 0.0)
    source, target = (va, va_strip), (vb, vb_strip)
    for count in range(21, 15, -1):
        finest_sweep(count, (kept, kept_strip), source, target, strips=count > 16)
        source, target = target, source

    def leave(local):
        out[local + place[0] * (15 - 2 * local)] = source[0][block(main_at(local + 1) + 8, 32)]

    each(16, leave, 4)


def call(kernel, inputs, outs, scratch):
    near = pl.BlockSpec(memory_space=pltpu.VMEM)
    return pl.pallas_call(
        kernel,
        out_shape=[jax.ShapeDtypeStruct(shape, jnp.float32) for shape in outs],
        in_specs=[near] * len(inputs),
        out_specs=[near] * len(outs),
        scratch_shapes=scratch,
        compiler_params=pltpu.CompilerParams(vmem_limit_bytes=VMEM_BYTES),
    )(*inputs)


def field(*shape):
    return pltpu.VMEM(shape, jnp.float32)


def from_sides(axis, to_first, to_second):
    size = lax.axis_size(axis)
    found = []
    for message, begin in ((to_second, 1), (to_first, 0)):
        lower = [(i, i + 1) for i in range(begin, size - 1, 2)]
        found.append(lax.ppermute(message, axis, lower + [(j, i) for i, j in lower]))
    return found[::-1]


def edge_rows(array, axis, last):
    odd = lax.axis_index(axis) % 2
    rows = array.shape[1]
    return lax.dynamic_slice_in_dim(array, (rows - 8) * (odd if last else 1 - odd), 8, 1)


def from_partner(message):
    return lax.ppermute(message, "gx", [(0, 1), (1, 0)])


def merged_sides(first, second):
    odd = lax.axis_index("gz") % 2 == 1
    above = lax.broadcasted_iota(jnp.int32, first.shape, first.ndim - 1) % 16 < 8
    return jnp.where(above == odd, second, first)


def fast_shards(source, conductivity):
    count_y, count_z = lax.axis_size("gy"), lax.axis_size("gz")
    own = jnp.concatenate([source, conductivity])
    message, to_first, to_second, *rows = call(
        pack_kernel,
        (own,),
        [(13, 32, 128), (2, 32, 128), (2, 32, 128), (32, 8, 128), (32, 8, 128)],
        [])
    partner = from_partner(message)
    strips = jnp.concatenate(from_sides("gz", to_first, to_second)[::-1])
    own_rev = from_sides("gy", *rows)[::-1]
    own_rev = lax.optimization_barrier(own_rev)
    own_rows = own_rev[::-1]
    strip_rows = from_sides("gy", *(edge_rows(strips, "gy", last) for last in (False, True)))
    message = jnp.concatenate(
        [strips[1].reshape(4, 8, 128), strips[3].reshape(4, 8, 128)]
        + [part for array in own_rows for part in (array[10:16], array[25:32])])
    beside = from_partner(message)
    strip_rows, _ = lax.optimization_barrier((strip_rows, message))
    corner = from_partner(jnp.concatenate([array[at : at + 1] for array in strip_rows for at in (1, 3)]))

    main, strip = field(MAIN, 128), field(STRIP, 128)
    kept = [(6, MAIN, 128), (7, STRIP, 128)]
    pre, lower, message, to_first, to_second, *kept0 = call(
        finest_kernel,
        (own, strips, *own_rows, *strip_rows, partner, beside, corner),
        [(16, 32, 128), (8, 16, 128), (40, 8, 128), (96, 128), (96, 128), *kept],
        [main, strip] * 4 + [main, field(512, 128)])
    partner = from_partner(message)
    strips = from_sides("gz", to_first, to_second)
    lower_strips = jnp.concatenate([part[:32].reshape(4, 8, 128) for part in strips])
    pre_strips = merged_sides(*(part[32:].reshape(2, 32, 128) for part in strips))
    further = from_partner(jnp.concatenate([lower_strips, pre_strips[0].reshape(4, 8, 128)]))
    flat = jnp.concatenate([lower.reshape(16, 8, 128), lower_strips, partner[:16], further[:8]])
    own2 = jnp.concatenate([pre, pre_strips, partner[16:].reshape(6, 32, 128), further[8:].reshape(1, 32, 128)])
    rows1 = from_sides("gy", *(jnp.concatenate([flat, edge_rows(own2, "gy", last)]) for last in (False, True)))

    window = field(SECOND, 128)
    share, *kept1 = call(
        second_kernel,
        (flat.reshape(24, 16, 128), *rows1),
        [(count_y * count_z, 4, 8, 128), (SECOND, 128), (5, SECOND, 128)],
        [window] * 4 + [field(256, 128)])
    shares = lax.all_to_all(share, ("gy", "gz"), 0, 0, tiled=True)

    scratch = whole_scratch(8, 32) + whole_scratch(4, 16) + whole_scratch(2, 8)
    scratch += [window, window] + [main, strip] * 2 + [field(8, 48, 128), field(384, 128), field(64, 128)]
    (result,) = call(
        functools.partial(last_kernel, count_y, count_z),
        (own2, *rows1, shares, *kept1, *kept0),
        [(16, 32, 128)],
        scratch)
    return result


def solution(mesh):
    in_specs = (P("gx", "gy", "gz"), P("gx", "gy", "gz"))
    out_specs = P("gx", "gy", "gz")

    def run(source, conductivity):
        counts = tuple(mesh.shape[axis] for axis in ("gx", "gy", "gz"))
        held = tuple(size // count for size, count in zip(source.shape, counts))
        fast = counts == (2, 4, 4) and held == (16, 32, 128)
        shards = fast_shards if fast else plain_shards
        return jax.shard_map(shards, mesh=mesh, in_specs=in_specs, out_specs=out_specs, check_vma=False)(source, conductivity)

    return run
```

```python
import functools

import jax
import jax.numpy as jnp
import numpy as np
from jax import lax
from jax.experimental import pallas as pl
from jax.experimental.pallas import tpu as pltpu
from jax.sharding import PartitionSpec as P

SWEEPS = 6
COARSE_SWEEPS = 16
DAMPING = 0.8
VMEM_BYTES = 32 * 2**20


def with_halo(array, sides, width):
    for axis, dim in sides:
        size, length = (lax.axis_size(axis), array.shape[dim])
        up = [(i, (i + 1) % size) for i in range(size - 1)]
        down = [(j, i) for i, j in up]
        last = lax.slice_in_dim(array, length - width, length, axis=dim)
        first = lax.slice_in_dim(array, 0, width, axis=dim)
        before = lax.ppermute(last, axis, up)
        after = lax.ppermute(first, axis, down)
        array = jnp.concatenate([before, array, after], axis=dim)
    return array


def centre(padded):
    return padded[1:-1, 1:-1, 1:-1]


def neighbours(padded):
    return [
        padded[2:, 1:-1, 1:-1],
        padded[:-2, 1:-1, 1:-1],
        padded[1:-1, 2:, 1:-1],
        padded[1:-1, :-2, 1:-1],
        padded[1:-1, 1:-1, 2:],
        padded[1:-1, 1:-1, :-2],
    ]


def zero_pad(field):
    return jnp.pad(field, 1)


def stencil(field_pad, coef_pad, weight):
    middle = centre(field_pad)
    coef_mid = centre(coef_pad)
    total = jnp.zeros_like(middle)
    for field_near, coef_near in zip(neighbours(field_pad), neighbours(coef_pad)):
        total = total + 0.5 * (coef_mid + coef_near) * (middle - field_near)
    return weight * total


def diagonal(coef_pad, weight):
    coef_mid = centre(coef_pad)
    total = jnp.zeros_like(coef_mid)
    for coef_near in neighbours(coef_pad):
        total = total + 0.5 * (coef_mid + coef_near)
    return weight * total


def restrict(field):
    shape = field.shape
    blocks = field.reshape(shape[0] // 2, 2, shape[1] // 2, 2, shape[2] // 2, 2)
    return blocks.mean(axis=(1, 3, 5))


def prolong(field):
    return jnp.repeat(jnp.repeat(jnp.repeat(field, 2, 0), 2, 1), 2, 2)


def jacobi(field, rhs_level, coef_pad, diag_terms, weight, padder):
    return field + DAMPING * (rhs_level - stencil(padder(field), coef_pad, weight)) / diag_terms


def face_rim(field):
    return with_halo(field, (("gx", 0), ("gy", 1), ("gz", 2)), 1)


def slab_pad(field):
    extended = with_halo(field, (("gx", 0),), 1)
    return jnp.pad(extended, ((0, 0), (1, 1), (1, 1)))


def single_sweeps(field, rhs_level, coef_pad, diag_terms, weight):
    for sweep_index in range(SWEEPS):
        field = jacobi(field, rhs_level, coef_pad, diag_terms, weight, face_rim)
    return field


def coarse_solve(rhs_level, coef_level):
    weight = 0.25**4
    coef_pad = zero_pad(coef_level)
    diag_terms = diagonal(coef_pad, weight)

    def coarse_step(count, field):
        return jacobi(field, rhs_level, coef_pad, diag_terms, weight, zero_pad)

    return lax.fori_loop(0, COARSE_SWEEPS, coarse_step, jnp.zeros_like(rhs_level))


def level_three(rhs_level, coef_level, padder, lower_solve):
    weight = 0.25**3
    coef_pad = padder(coef_level)
    diag_terms = diagonal(coef_pad, weight)
    field = jnp.zeros_like(rhs_level)
    for sweep_index in range(SWEEPS):
        field = jacobi(field, rhs_level, coef_pad, diag_terms, weight, padder)
    residual = rhs_level - stencil(padder(field), coef_pad, weight)
    field = field + prolong(lower_solve(restrict(residual), restrict(coef_level)))
    for sweep_index in range(SWEEPS):
        field = jacobi(field, rhs_level, coef_pad, diag_terms, weight, padder)
    return field


def plain_shards(source, conductivity):
    count_x, count_y, count_z = (lax.axis_size("gx"), lax.axis_size("gy"), lax.axis_size("gz"))
    place_x, place_y, place_z = (lax.axis_index("gx"), lax.axis_index("gy"), lax.axis_index("gz"))
    rhs_level = source
    coef_level = conductivity
    saved = []
    for level_index in range(3):
        weight = 0.25**level_index
        coef_pad = face_rim(coef_level)
        diag_terms = diagonal(coef_pad, weight)
        extras = None
        field = single_sweeps(jnp.zeros_like(rhs_level), rhs_level, coef_pad, diag_terms, weight)
        residual = rhs_level - stencil(face_rim(field), coef_pad, weight)
        saved.append((field, rhs_level, coef_pad, diag_terms, weight, extras))
        rhs_level = restrict(residual)
        coef_level = restrict(coef_level)
    rows_x, rows_y, rows_z = rhs_level.shape
    stacked = jnp.stack([rhs_level, coef_level])[None]
    gathered = lax.all_gather(stacked, ("gy", "gz"), axis=0, tiled=True)
    slab = gathered.reshape(count_y, count_z, 2, rows_x, rows_y, rows_z)
    slab = slab.transpose(2, 3, 0, 4, 1, 5).reshape(2, rows_x, count_y * rows_y, count_z * rows_z)

    def lower_groups(rhs_low, coef_low):
        lowered = lax.all_gather(jnp.stack([rhs_low, coef_low]), "gx", axis=1, tiled=True)
        whole = coarse_solve(lowered[0], lowered[1])
        return lax.dynamic_slice_in_dim(whole, place_x * (rows_x // 2), rows_x // 2, 0)

    field = level_three(slab[0], slab[1], slab_pad, lower_groups)
    field = lax.dynamic_slice_in_dim(field, place_y * rows_y, rows_y, 1)
    result = lax.dynamic_slice_in_dim(field, place_z * rows_z, rows_z, 2)
    for level_index in (2, 1, 0):
        field, rhs_here, coef_pad, diag_terms, weight, extras = saved[level_index]
        field = field + prolong(result)
        field = single_sweeps(field, rhs_here, coef_pad, diag_terms, weight)
        result = field
    return result


ROWS = 48
MARGIN = 8
MAIN = MARGIN + 25 * ROWS + MARGIN
STRIP = MARGIN + 5 * ROWS + MARGIN
SECOND = MARGIN + 18 * ROWS + MARGIN


def roll(value, shift, axis):
    if isinstance(shift, int):
        shift = shift % value.shape[axis]
        if shift == 0:
            return value
    return pltpu.roll(value, shift, axis)


def iota(shape, axis):
    return lax.broadcasted_iota(jnp.int32, shape, axis)


def gather_lanes(value, lanes):
    return jnp.take_along_axis(value, lanes, axis=1, mode="promise_in_bounds")


def block(at, count):
    return pl.ds(pl.multiple_of(at, 8) if not isinstance(at, int) else at, count)


def terms(coef, nears, rhs, weight):
    faces = [0.5 * (coef + near) for near in nears]
    total = functools.reduce(lambda a, b: a + b, faces)
    scale = jnp.where(coef > 0.0, DAMPING / total, 0.0)
    return faces, scale, rhs * scale * (1.0 / weight), total * (weight / DAMPING)


def each(count, body, step):
    def several(turn, carry):
        for ahead in range(step):
            body(turn * step + ahead)
        return carry

    def single(index, carry):
        body(index)
        return carry

    whole = count // step
    lax.fori_loop(0, whole, several, 0)
    if count % step:
        lax.fori_loop(whole * step, count, single, 0)


def row_pairs(array, rows):
    return array[pl.ds(0, rows // 2, stride=2), :] + array[pl.ds(1, rows // 2, stride=2), :]


def repeat_rows(array, value):
    rows = value.shape[0]
    array[pl.ds(0, rows, stride=2), :] = value
    array[pl.ds(1, rows, stride=2), :] = value


def lane_pairs(value):
    return value + roll(value, -1, 1)


def both_ways(face, value, axis):
    return face * roll(value, -1, axis) + roll(face * value, 1, axis)


def by_side(swapped, odd):
    first, second = swapped
    return jnp.where(odd, first, second), jnp.where(odd, second, first)


def device_place():
    return [lax.axis_index(axis) for axis in ("gx", "gy", "gz")]


def odd_at(place, axis):
    return (place[axis] & 1) == 1


def with_tiles(middle, first, second, odd):
    sides = [by_side(tiles, odd) for tiles in zip(first, second)]
    return jnp.concatenate([low for low, _ in sides] + list(middle) + [high for _, high in sides], axis=0)


def main_at(plane):
    return MARGIN + ROWS * plane


def joined(middle, edge):
    lane = iota(middle.shape, 1)
    return jnp.where(lane == 127, edge, roll(middle, -1, 1)), jnp.where(lane == 0, edge, roll(middle, 1, 1))


def facing(own, plane, slot):
    lane = iota(own.shape, 1)
    return jnp.where((lane == 16 * slot + 7) | (lane == 16 * slot + 8), roll(plane, 16 * slot + 8, 1), own)


def strip_nears(strip, own, group):
    at = main_at(group + 1)
    middle = strip[block(at, ROWS)]
    lane = iota((ROWS, 128), 1)
    slot_lane = lane & 15
    further = jnp.where(lane < 112, roll(middle, -16, 1), roll(strip[block(at + ROWS, ROWS)], -16, 1))
    nearer = jnp.where(lane >= 16, roll(middle, 16, 1), roll(strip[block(at - ROWS, ROWS)], 16, 1))
    after = jnp.where(slot_lane == 7, own, roll(middle, -1, 1))
    before = jnp.where(slot_lane == 8, own, roll(middle, 1, 1))
    return middle, [further, nearer, roll(middle, -1, 0), roll(middle, 1, 0), after, before]


def finest_terms(rhs, coef, kept, inverse):
    main, strip = coef

    def group(index, slots):
        first = 8 * index + 1
        before = main[block(main_at(first - 1), ROWS)]
        here = main[block(main_at(first), ROWS)]
        held = strip[block(main_at(index + 1), ROWS)]
        own = jnp.zeros((ROWS, 128), jnp.float32)
        for slot in range(slots):
            at = block(main_at(first + slot), ROWS)
            after = main[block(main_at(first + slot + 1), ROWS)]
            nears = [after, before, roll(here, -1, 0), roll(here, 1, 0), *joined(here, roll(held, 120 - 16 * slot, 1))]
            faces, scale, start, back = terms(here, nears, rhs[0][at], 1.0)
            for side, value in enumerate((faces[0], faces[2], faces[4], faces[5], scale, start)):
                kept[0][side, at] = value
            inverse[at] = back
            own = facing(own, here, slot)
            before, here = here, after
        for slot in range(slots, 8):
            own = facing(own, main[block(main_at(first + slot), ROWS)], slot)
        at = block(main_at(index + 1), ROWS)
        middle, nears = strip_nears(strip, own, index)
        faces, scale, start, _ = terms(middle, nears, rhs[1][at], 1.0)
        for side in range(6):
            kept[1][side, at] = faces[side] * scale
        kept[1][6, at] = start

    each(2, lambda index: group(index, 8), 1)
    group(2, 6)


def finest_sweep(count, kept, source, target, keep=1.0 - DAMPING, strips=True):
    main, strip = source

    def group(index, slots):
        first = 8 * index + 1
        at = block(main_at(first - 1), ROWS)
        flux = kept[0][0, at] * main[at]
        here = main[block(main_at(first), ROWS)]
        held = strip[block(main_at(index + 1), ROWS)]
        own = jnp.zeros((ROWS, 128), jnp.float32)
        for slot in range(slots):
            at = block(main_at(first + slot), ROWS)
            after = main[block(main_at(first + slot + 1), ROWS)]
            face = kept[0][0, at]
            total = flux + face * after
            flux = face * here
            total = total + both_ways(kept[0][1, at], here, 0)
            above, below = joined(here, roll(held, 120 - 16 * slot, 1))
            total = total + kept[0][2, at] * above + kept[0][3, at] * below
            target[0][at] = kept[0][5, at] + keep * here + kept[0][4, at] * total
            if strips:
                own = facing(own, here, slot)
            here = after
        if strips:
            at = block(main_at(index + 1), ROWS)
            middle, nears = strip_nears(strip, own, index)
            total = kept[1][6, at] + keep * middle
            for side, near in enumerate(nears):
                total = total + kept[1][side, at] * near
            target[1][at] = total

    each(2, lambda index: group(index, 8), 1)
    if count > 16:
        group(2, count - 16)


def strip_pages(rhs_planes, coef_planes):
    lane = iota((32, 128), 1)
    left = jnp.zeros((32, 128), jnp.float32)
    right = jnp.zeros((32, 128), jnp.float32)
    for field_at, planes in ((0, rhs_planes), (8, coef_planes)):
        for slot, plane in enumerate(planes):
            at = 16 * slot + field_at
            inside = (lane >= at) & (lane < at + 8)
            left = jnp.where(inside, gather_lanes(plane, 7 - (lane & 7)), left)
            right = jnp.where(inside, gather_lanes(plane, 127 - (lane & 7)), right)
    return left, right


def pack_kernel(own, message, to_first, to_second, rows_first, rows_second):
    place = device_place()
    odd, odd_y = odd_at(place, 2), odd_at(place, 1)
    for group in range(2):
        planes = ([], [])
        for local in range(8 * group, 8 * group + 8):
            held = local + place[0] * (15 - 2 * local)
            for field_at in range(2):
                plane = own[16 * field_at + held]
                at = 16 * field_at + local
                rows_first[at], rows_second[at] = by_side((plane[0:8], plane[24:32]), odd_y)
                if local > 9 - field_at:
                    message[6 * field_at + 15 - local] = plane
                planes[field_at].append(plane)
        to_first[group], to_second[group] = by_side(strip_pages(*planes), odd)


def mirrored_slots(value):
    lane = iota(value.shape, 1)
    found = value
    for slot in range(8):
        inside = (lane >= 16 * slot) & (lane < 16 * slot + 16)
        found = jnp.where(inside, roll(value, 16 * (2 * slot - 7), 1), found)
    return found


def finest_kernel(own, strips, own_first, own_second, strip_first, strip_second, partner, beside, corner, pre, lower, message,
                  to_first, to_second, kept, kept_strip, rhs, rhs_strip, coef, coef_strip, va, va_strip, vb, vb_strip, inverse,
                  sums):
    place = device_place()
    blank = jnp.zeros((ROWS, 128), jnp.float32)
    outside = block(main_at(0), ROWS)
    for array in (coef, va, vb):
        array[outside] = blank
    coef[block(main_at(24), ROWS)] = blank
    kept[0, outside] = blank
    kept[5, outside] = blank
    for array in (coef_strip, va_strip, vb_strip, kept_strip.at[6]):
        array[outside] = blank
        array[block(main_at(4), ROWS)] = blank
    odd_y, odd_z = odd_at(place, 1), odd_at(place, 2)

    no_rows = jnp.zeros((8, 128), jnp.float32)
    for local in range(23):
        at = block(main_at(local + 1), ROWS)
        for field_at, array in enumerate((rhs, coef)):
            if local < 16:
                page = 16 * field_at + local
                held = 16 * field_at + local + place[0] * (15 - 2 * local)
                array[at] = with_tiles([own[held]], [own_first[page]], [own_second[page]], odd_y)
            elif local < 22 + field_at:
                step = local - 16
                page = 12 + 6 * field_at - step
                beyond = step == 5 + field_at
                first, second = (no_rows, no_rows) if beyond else (beside[page], beside[11 + page])
                array[at] = with_tiles([partner[6 * field_at + step]], [first], [second], odd_y)
    above = (iota((ROWS, 128), 1) & 15) < 8
    for group in range(3):
        pages = []
        for which in range(2):
            if group < 2:
                page = 2 - 2 * which + group
                pages.append(with_tiles([strips[page]], [strip_first[page]], [strip_second[page]], odd_y))
            else:
                tiles = [beside[4 - 4 * which + part] for part in range(4)]
                pages.append(with_tiles(tiles, [corner[1 - which]], [corner[3 - which]], odd_y))
        left, right = by_side(pages, odd_z)
        if group == 2:
            left, right = mirrored_slots(left), mirrored_slots(right)
        at = block(main_at(group + 1), ROWS)
        rhs_strip[at] = jnp.where(above, right, roll(left, 8, 1))
        coef_strip[at] = jnp.where(above, roll(right, -8, 1), left)
    both = (kept, kept_strip)
    finest_terms((rhs, rhs_strip), (coef, coef_strip), both, inverse)
    a, b = (va, va_strip), (vb, vb_strip)
    source = (kept.at[5], kept_strip.at[6])
    for count, target in zip(range(21, 16, -1), (a, b, a, b, a)):
        finest_sweep(count, both, source, target)
        source = target
    finest_sweep(16, both, a, b, -DAMPING, False)

    def pair(index):
        total = jnp.zeros((32, 128), jnp.float32)
        conduct = jnp.zeros((32, 128), jnp.float32)
        for local in (2 * index, 2 * index + 1):
            at = block(main_at(local + 1) + 8, 32)
            value = va[at]
            pre[local] = value
            total = total + vb[at] * inverse[at]
            conduct = conduct + coef[at]
        sums[block(index * 32, 32)] = total
        sums[block(index * 32 + 256, 32)] = conduct

    each(8, pair, 4)
    folded = lane_pairs(row_pairs(sums, 512)) * 0.125
    lane = iota((128, 128), 1)
    merged = jnp.where(lane < 64, gather_lanes(folded[0:128], (2 * lane) & 127), gather_lanes(folded[128:256], (2 * lane) & 127))
    lane = iota((16, 128), 1)
    for group in range(2):
        right = jnp.zeros((16, 128), jnp.float32)
        left = jnp.zeros((16, 128), jnp.float32)
        for slot in range(4):
            local = 4 * group + slot
            plane = merged[16 * local : 16 * local + 16]
            lower[local] = plane
            message[2 * local] = plane[0:8]
            message[2 * local + 1] = plane[8:16]
            for field_at in range(2):
                at = 32 * slot + 16 * field_at
                inside = (lane >= at) & (lane < at + 16)
                right = jnp.where(inside, roll(plane, at - 48 - 64 * field_at, 1), right)
                left = jnp.where(inside, roll(plane, at - 64 * field_at, 1), left)
        rows = slice(16 * group, 16 * group + 16)
        to_first[rows], to_second[rows] = by_side((left, right), odd_z)
    lane = iota((32, 128), 1)
    mirrored = jnp.where((lane & 15) < 8, 7 - (lane & 15), 135 - (lane & 15))
    for local in range(10, 16):
        for part in range(4):
            message[4 * local - 24 + part] = pre[local, 8 * part : 8 * part + 8]
    for group in range(2):
        value = jnp.zeros((32, 128), jnp.float32)
        for slot in range(8):
            inside = (lane >= 16 * slot) & (lane < 16 * slot + 16)
            value = jnp.where(inside, gather_lanes(pre[8 * group + slot], mirrored), value)
        rows = slice(64 - 32 * group, 96 - 32 * group)
        to_first[rows] = value
        to_second[rows] = value


def second_window(place, own, first, second, rhs, coef):
    lane = iota((ROWS, 128), 1)
    odd_y, odd_z = odd_at(place, 1), odd_at(place, 2)

    def page(index):
        low, high = by_side((first[2 * index], second[2 * index]), odd_y)
        low_next, high_next = by_side((first[2 * index + 1], second[2 * index + 1]), odd_y)
        return jnp.concatenate([low, low_next, own[index], high, high_next], axis=0)

    for group in range(4):
        at = (8 + group) if group < 2 else 18 + group
        left, right = by_side((page(at), page(at + 2)), odd_z)
        for slot in range(4):
            other = 4 * group + slot
            local, middle = (other, page(other)) if group < 2 else (23 - other, page(4 + other))
            for field_at, array in enumerate((rhs, coef)):
                at = 32 * slot + 16 * field_at
                value = jnp.where(lane < 64, roll(middle, -64 * field_at, 1), 0.0)
                value = jnp.where((lane >= 64) & (lane < 80), roll(right, 64 - at, 1), value)
                array[block(main_at(local + 1), ROWS)] = jnp.where(lane >= 112, roll(left, 112 - at, 1), value)


def second_sweep(count, kept, source, target, skip=0, keep=1.0 - DAMPING):
    rows = ROWS - 2 * skip
    at = block(main_at(0) + skip, rows)
    flux = kept[0, at] * source[at]
    here = source[block(main_at(1) + skip, rows)]
    for plane in range(1, count + 1):
        at = block(main_at(plane) + skip, rows)
        after = source[block(main_at(plane + 1) + skip, rows)]
        face = kept[0, at]
        total = flux + face * after
        flux = face * here
        total = total + both_ways(kept[1, at], here, 0) + both_ways(kept[2, at], here, 1)
        target[at] = kept[4, at] + keep * here + kept[3, at] * total
        here = after


def second_kernel(own, first, second, share, va, kept, rhs, coef, inverse, vb, sums):
    place = device_place()
    blank = jnp.zeros((ROWS, 128), jnp.float32)
    for plane in (0, 17):
        at = block(main_at(plane), ROWS)
        for array in (coef, va, vb, kept.at[0], kept.at[4]):
            array[at] = blank
    second_window(place, own, first, second, rhs, coef)

    def plane(index):
        at = block(main_at(index + 1), ROWS)
        here = coef[at]
        nears = [coef[block(main_at(index + 2), ROWS)], coef[block(main_at(index), ROWS)],
                 roll(here, -1, 0), roll(here, 1, 0), roll(here, -1, 1), roll(here, 1, 1)]
        faces, scale, start, inverse[at] = terms(here, nears, rhs[at], 0.25)
        for side, value in enumerate((faces[0], faces[2], faces[4], scale, start)):
            kept[side, at] = value

    each(16, plane, 4)
    second_sweep(16, kept, kept.at[4], va)

    def twice(index, carry):
        second_sweep(16, kept, va, vb)
        second_sweep(16, kept, vb, va)
        return carry

    lax.fori_loop(0, 2, twice, 0)
    second_sweep(16, kept, va, vb, 8, -DAMPING)
    for local in range(8):
        residual = jnp.zeros((16, 128), jnp.float32)
        conduct = jnp.zeros((16, 128), jnp.float32)
        for here in (2 * local + 1, 2 * local + 2):
            at = block(main_at(here) + 16, 16)
            residual = residual + vb[at] * inverse[at]
            conduct = conduct + coef[at]
        sums[16 * local : 16 * local + 16] = residual
        sums[128 + 16 * local : 144 + 16 * local] = conduct
    folded = lane_pairs(row_pairs(sums, 256)) * 0.125
    lane = iota((8, 128), 1)
    for group in range(4):
        value = jnp.zeros((8, 128), jnp.float32)
        for plane in range(2):
            for field_at in range(2):
                row = 64 * field_at + 8 * (2 * group + plane)
                at = 64 * plane + 32 * field_at
                inside = (lane >= at) & (lane < at + 32)
                value = jnp.where(inside, gather_lanes(folded[row : row + 8], (2 * lane) & 63), value)
        for device in range(share.shape[0]):
            share[device, group] = value


def whole_terms(planes, rows, lanes, rhs, coef, kept, weight):
    row = iota((rows, 128), 0)
    lane = iota((rows, 128), 1)
    outside = jnp.zeros((rows, 128), jnp.float32)
    held = [outside] + [coef[here] for here in range(planes)] + [outside]
    for here in range(planes):
        middle = held[here + 1]
        nears = [
            held[here + 2], held[here],
            jnp.where(row == rows - 1, 0.0, roll(middle, -1, 0)), jnp.where(row == 0, 0.0, roll(middle, 1, 0)),
            jnp.where(lane >= lanes - 1, 0.0, roll(middle, -1, 1)), jnp.where(lane == 0, 0.0, roll(middle, 1, 1))]
        faces, scale, start, back = terms(middle, nears, rhs[here], weight)
        for side in range(3):
            kept[side, here] = jnp.where(nears[2 * side] > 0.0, faces[2 * side], 0.0)
        kept[3, here] = scale
        kept[4, here] = start
        kept[5, here] = back


def whole_change(kept, values, keep):
    found = []
    flux = None
    for here, value in enumerate(values):
        total = both_ways(kept[1, here], value, 0) + both_ways(kept[2, here], value, 1)
        if here > 0:
            total = total + flux
        if here + 1 < len(values):
            face = kept[0, here]
            total = total + face * values[here + 1]
            flux = face * value
        found.append(kept[4, here] + keep * value + kept[3, here] * total)
    return tuple(found)


def whole_sweeps(count, kept, values):
    return lax.fori_loop(0, count, lambda index, held: whole_change(kept, held, 1.0 - DAMPING), tuple(values))


def whole_solve(level, scratch):
    kept, rhs, coef, rows_of = scratch[0]
    planes, rows = rhs.shape[0], rhs.shape[1]
    lanes = 128 >> (level - 2)
    whole_terms(planes, rows, lanes, rhs, coef, kept, 0.25**level)
    start = [kept[4, here] for here in range(planes)]
    values = whole_sweeps((COARSE_SWEEPS if level == 4 else SWEEPS) - 1, kept, start)
    if level < 4:
        residual = [value * kept[5, here] for here, value in enumerate(whole_change(kept, values, -DAMPING))]
        size = planes // 2 * rows
        for pair in range(planes // 2):
            at = pair * rows
            rows_of[at : at + rows] = residual[2 * pair] + residual[2 * pair + 1]
            rows_of[size + at : size + at + rows] = coef[2 * pair] + coef[2 * pair + 1]
        folded = lane_pairs(row_pairs(rows_of, 2 * size)) * 0.125
        lane = iota(folded.shape, 1)
        folded = jnp.where(lane < lanes // 2, gather_lanes(folded, (2 * lane) & 127), 0.0)
        half = rows // 2
        for pair in range(planes // 2):
            scratch[1][1][pair] = folded[pair * half : pair * half + half]
            scratch[1][2][pair] = folded[size // 2 + pair * half : size // 2 + pair * half + half]
        lower = jnp.concatenate(whole_solve(level + 1, scratch[1:]), axis=0)
        repeat_rows(rows_of.at[0:size], gather_lanes(lower, lax.shift_right_logical(iota(lower.shape, 1), 1)))
        values = [
            value + rows_of[here // 2 * rows : here // 2 * rows + rows] for here, value in enumerate(values)]
        values = whole_sweeps(SWEEPS, kept, values)
    return list(values)


def whole_scratch(planes, rows):
    return [field(6, planes, rows, 128), field(planes, rows, 128), field(planes, rows, 128), field(planes * rows, 128)]


def third_whole(shares, count_y, count_z, rhs, coef):
    lane = iota((8, 128), 1)
    width = 128 // count_z
    for local in range(8):
        for at_y in range(count_y):
            for index, array in enumerate((rhs, coef)):
                value = jnp.zeros((8, 128), jnp.float32)
                for at_z in range(count_z):
                    held = shares[at_y * count_z + at_z, local // 2]
                    at = 64 * (local % 2) + 32 * index
                    inside = (lane >= width * at_z) & (lane < width * at_z + width)
                    value = jnp.where(inside, roll(held, width * at_z - at, 1), value)
                array[local, 8 * at_y : 8 * at_y + 8] = value


def last_kernel(count_y, count_z, own2, first1, second1, shares, pre1, kept1, kept, kept_strip, out, *scratch):
    place = device_place()
    deep = [scratch[0:4], scratch[4:8], scratch[8:12]]
    va1, vb1, va, va_strip, vb, vb_strip = scratch[12:18]
    framed, twice1, twice0 = scratch[18:21]
    third_whole(shares, count_y, count_z, deep[0][1], deep[0][2])
    third = whole_solve(2, deep)

    blank = jnp.zeros((ROWS, 128), jnp.float32)
    for array, outer in ((va1, 17), (va_strip, 4), (vb_strip, 4)):
        array[block(main_at(outer), ROWS)] = blank
    for array in (va1, va, va_strip, vb, vb_strip):
        array[block(main_at(0), ROWS)] = blank
    rows = third[0].shape[0]
    for index, plane in enumerate(third):
        framed[index, 0:8] = blank[0:8]
        framed[index, 8 : 8 + rows] = plane
        framed[index, 8 + rows : 16 + rows] = blank[0:8]
    for index in range(8):
        near = framed[index, pl.ds(pl.multiple_of(8 * place[1], 8), 24), :]
        repeat_rows(twice1.at[48 * index : 48 * index + 48], near)
    lane = iota((ROWS, 128), 1)
    held = lax.shift_right_arithmetic(jnp.where(lane < 96, lane, lane - 128), 1) + 32 * place[2]
    inside = (held >= 0) & (held < 128) & ((lane < 80) | (lane >= 112))
    for index in range(8):
        wide = jnp.where(inside, gather_lanes(twice1[48 * index : 48 * index + 48], held & 127), 0.0)
        for here in (2 * index + 1, 2 * index + 2):
            there = block(main_at(here), ROWS)
            va1[there] = pre1[there] + jnp.where(kept1[3, there] > 0.0, wide, 0.0)
    vb1[block(main_at(0), ROWS)] = blank
    vb1[block(main_at(17), ROWS)] = blank
    source, target = va1, vb1
    for sweep in range(SWEEPS):
        second_sweep(16 - sweep, kept1, source, target, 8 if sweep else 0)
        source, target = target, source

    odd_y = odd_at(place, 1)

    def page(index):
        low, high = by_side((first1[48 + index], second1[48 + index]), odd_y)
        return jnp.concatenate([low, own2[index], high], axis=0)

    slot_lane = lane & 15
    above = slot_lane < 8
    facing_lane = jnp.where(above, 64 + lax.shift_right_logical(7 - slot_lane, 1), 127 - lax.shift_right_logical(slot_lane - 8, 1))
    for group in range(3):
        more = jnp.zeros((ROWS, 128), jnp.float32)
        for index in range(4 * group, min(4 * group + 4, 11)):
            at = main_at(index + 1) + 8
            repeat_rows(twice0, source[at : at + 32])
            near = twice0[8:56]
            wide = gather_lanes(near, lax.shift_right_logical(lane, 1))
            at = 32 * (index - 4 * group)
            more = jnp.where((lane >= at) & (lane < at + 32), gather_lanes(near, facing_lane & 127), more)
            for local in (2 * index, 2 * index + 1):
                there = block(main_at(local + 1), ROWS)
                middle = page(local if local < 16 else 39 - local)
                va[there] = middle + jnp.where(kept[4, there] > 0.0, wide, 0.0)
        value = mirrored_slots(page(24)) if group == 2 else page(17 - group)
        there = block(main_at(group + 1), ROWS)
        va_strip[there] = value + jnp.where(kept_strip[0, there] > 0.0, more, 0.0)
    source, target = (va, va_strip), (vb, vb_strip)
    for count in range(21, 15, -1):
        finest_sweep(count, (kept, kept_strip), source, target, strips=count > 16)
        source, target = target, source

    def leave(local):
        out[local + place[0] * (15 - 2 * local)] = source[0][block(main_at(local + 1) + 8, 32)]

    each(16, leave, 4)


def call(kernel, inputs, outs, scratch):
    near = pl.BlockSpec(memory_space=pltpu.VMEM)
    return pl.pallas_call(
        kernel,
        out_shape=[jax.ShapeDtypeStruct(shape, jnp.float32) for shape in outs],
        in_specs=[near] * len(inputs),
        out_specs=[near] * len(outs),
        scratch_shapes=scratch,
        compiler_params=pltpu.CompilerParams(vmem_limit_bytes=VMEM_BYTES),
    )(*inputs)


def field(*shape):
    return pltpu.VMEM(shape, jnp.float32)


def from_sides(axis, to_first, to_second):
    size = lax.axis_size(axis)
    found = []
    for message, begin in ((to_second, 1), (to_first, 0)):
        lower = [(i, i + 1) for i in range(begin, size - 1, 2)]
        found.append(lax.ppermute(message, axis, lower + [(j, i) for i, j in lower]))
    return found[::-1]


def edge_rows(array, axis, last):
    odd = lax.axis_index(axis) % 2
    rows = array.shape[1]
    return lax.dynamic_slice_in_dim(array, (rows - 8) * (odd if last else 1 - odd), 8, 1)


def from_partner(message):
    return lax.ppermute(message, "gx", [(0, 1), (1, 0)])


def merged_sides(first, second):
    odd = lax.axis_index("gz") % 2 == 1
    above = np.arange(128) % 16 < 8
    return jnp.where(above == odd, second, first)


def fast_shards(source, conductivity):
    count_y, count_z = lax.axis_size("gy"), lax.axis_size("gz")
    second = np.array([False, True]).reshape(2, 1, 1, 1)
    own = jnp.where(second, conductivity[None], source[None]).reshape(32, 32, 128)
    message, to_first, to_second, *rows = call(
        pack_kernel,
        (own,),
        [(13, 32, 128), (2, 32, 128), (2, 32, 128), (32, 8, 128), (32, 8, 128)],
        [])
    partner = from_partner(message)
    strips = jnp.concatenate(from_sides("gz", to_first, to_second)[::-1])
    own_rev = from_sides("gy", *rows)[::-1]
    own_rev = lax.optimization_barrier(own_rev)
    own_rows = own_rev[::-1]
    strip_rows = from_sides("gy", *(edge_rows(strips, "gy", last) for last in (False, True)))
    message = jnp.concatenate(
        [strips[1].reshape(4, 8, 128), strips[3].reshape(4, 8, 128)]
        + [part for array in own_rows for part in (array[11:16], array[26:32])])
    beside = from_partner(message)
    strip_rows, _ = lax.optimization_barrier((strip_rows, message))
    corner = from_partner(jnp.concatenate([array[at : at + 1] for array in strip_rows for at in (1, 3)]))

    main, strip = field(MAIN, 128), field(STRIP, 128)
    kept = [(6, MAIN, 128), (7, STRIP, 128)]
    pre, lower, message, to_first, to_second, *kept0 = call(
        finest_kernel,
        (own, strips, *own_rows, *strip_rows, partner, beside, corner),
        [(16, 32, 128), (8, 16, 128), (40, 8, 128), (96, 128), (96, 128), *kept],
        [main, strip] * 4 + [main, field(512, 128)])
    partner = from_partner(message)
    strips = from_sides("gz", to_first, to_second)
    lower_strips = jnp.concatenate([part[:32].reshape(4, 8, 128) for part in strips])
    pre_strips = merged_sides(*(part[32:].reshape(2, 32, 128) for part in strips))
    further = from_partner(jnp.concatenate([lower_strips, pre_strips[0].reshape(4, 8, 128)]))
    flat = jnp.concatenate([lower.reshape(16, 8, 128), lower_strips, partner[:16], further[:8]])
    own2 = jnp.concatenate([pre, pre_strips, partner[16:].reshape(6, 32, 128), further[8:].reshape(1, 32, 128)])
    rows1 = from_sides("gy", *(jnp.concatenate([flat, edge_rows(own2, "gy", last)]) for last in (False, True)))

    window = field(SECOND, 128)
    share, *kept1 = call(
        second_kernel,
        (flat.reshape(24, 16, 128), *rows1),
        [(count_y * count_z, 4, 8, 128), (SECOND, 128), (5, SECOND, 128)],
        [window] * 4 + [field(256, 128)])
    shares = lax.all_to_all(share, ("gy", "gz"), 0, 0, tiled=True)

    scratch = whole_scratch(8, 32) + whole_scratch(4, 16) + whole_scratch(2, 8)
    scratch += [window, window] + [main, strip] * 2 + [field(8, 48, 128), field(384, 128), field(64, 128)]
    (result,) = call(
        functools.partial(last_kernel, count_y, count_z),
        (own2, *rows1, shares, *kept1, *kept0),
        [(16, 32, 128)],
        scratch)
    return result


def solution(mesh):
    in_specs = (P("gx", "gy", "gz"), P("gx", "gy", "gz"))
    out_specs = P("gx", "gy", "gz")

    def run(source, conductivity):
        counts = tuple(mesh.shape[axis] for axis in ("gx", "gy", "gz"))
        held = tuple(size // count for size, count in zip(source.shape, counts))
        fast = counts == (2, 4, 4) and held == (16, 32, 128)
        shards = fast_shards if fast else plain_shards
        return jax.shard_map(shards, mesh=mesh, in_specs=in_specs, out_specs=out_specs, check_vma=False)(source, conductivity)

    return run
```

```python
import functools

import jax
import jax.numpy as jnp
from jax import lax
from jax.experimental import pallas as pl
from jax.experimental.pallas import tpu as pltpu
from jax.sharding import PartitionSpec as P

SWEEPS = 6
COARSE_SWEEPS = 16
DAMPING = 0.8
VMEM_BYTES = 32 * 2**20


def with_halo(array, sides, width):
    for axis, dim in sides:
        size, length = (lax.axis_size(axis), array.shape[dim])
        up = [(i, (i + 1) % size) for i in range(size - 1)]
        down = [(j, i) for i, j in up]
        last = lax.slice_in_dim(array, length - width, length, axis=dim)
        first = lax.slice_in_dim(array, 0, width, axis=dim)
        before = lax.ppermute(last, axis, up)
        after = lax.ppermute(first, axis, down)
        array = jnp.concatenate([before, array, after], axis=dim)
    return array


def centre(padded):
    return padded[1:-1, 1:-1, 1:-1]


def neighbours(padded):
    return [
        padded[2:, 1:-1, 1:-1],
        padded[:-2, 1:-1, 1:-1],
        padded[1:-1, 2:, 1:-1],
        padded[1:-1, :-2, 1:-1],
        padded[1:-1, 1:-1, 2:],
        padded[1:-1, 1:-1, :-2],
    ]


def zero_pad(field):
    return jnp.pad(field, 1)


def stencil(field_pad, coef_pad, weight):
    middle = centre(field_pad)
    coef_mid = centre(coef_pad)
    total = jnp.zeros_like(middle)
    for field_near, coef_near in zip(neighbours(field_pad), neighbours(coef_pad)):
        total = total + 0.5 * (coef_mid + coef_near) * (middle - field_near)
    return weight * total


def diagonal(coef_pad, weight):
    coef_mid = centre(coef_pad)
    total = jnp.zeros_like(coef_mid)
    for coef_near in neighbours(coef_pad):
        total = total + 0.5 * (coef_mid + coef_near)
    return weight * total


def restrict(field):
    shape = field.shape
    blocks = field.reshape(shape[0] // 2, 2, shape[1] // 2, 2, shape[2] // 2, 2)
    return blocks.mean(axis=(1, 3, 5))


def prolong(field):
    return jnp.repeat(jnp.repeat(jnp.repeat(field, 2, 0), 2, 1), 2, 2)


def jacobi(field, rhs_level, coef_pad, diag_terms, weight, padder):
    return field + DAMPING * (rhs_level - stencil(padder(field), coef_pad, weight)) / diag_terms


def face_rim(field):
    return with_halo(field, (("gx", 0), ("gy", 1), ("gz", 2)), 1)


def slab_pad(field):
    extended = with_halo(field, (("gx", 0),), 1)
    return jnp.pad(extended, ((0, 0), (1, 1), (1, 1)))


def single_sweeps(field, rhs_level, coef_pad, diag_terms, weight):
    for sweep_index in range(SWEEPS):
        field = jacobi(field, rhs_level, coef_pad, diag_terms, weight, face_rim)
    return field


def coarse_solve(rhs_level, coef_level):
    weight = 0.25**4
    coef_pad = zero_pad(coef_level)
    diag_terms = diagonal(coef_pad, weight)

    def coarse_step(count, field):
        return jacobi(field, rhs_level, coef_pad, diag_terms, weight, zero_pad)

    return lax.fori_loop(0, COARSE_SWEEPS, coarse_step, jnp.zeros_like(rhs_level))


def level_three(rhs_level, coef_level, padder, lower_solve):
    weight = 0.25**3
    coef_pad = padder(coef_level)
    diag_terms = diagonal(coef_pad, weight)
    field = jnp.zeros_like(rhs_level)
    for sweep_index in range(SWEEPS):
        field = jacobi(field, rhs_level, coef_pad, diag_terms, weight, padder)
    residual = rhs_level - stencil(padder(field), coef_pad, weight)
    field = field + prolong(lower_solve(restrict(residual), restrict(coef_level)))
    for sweep_index in range(SWEEPS):
        field = jacobi(field, rhs_level, coef_pad, diag_terms, weight, padder)
    return field


def plain_shards(source, conductivity):
    count_x, count_y, count_z = (lax.axis_size("gx"), lax.axis_size("gy"), lax.axis_size("gz"))
    place_x, place_y, place_z = (lax.axis_index("gx"), lax.axis_index("gy"), lax.axis_index("gz"))
    rhs_level = source
    coef_level = conductivity
    saved = []
    for level_index in range(3):
        weight = 0.25**level_index
        coef_pad = face_rim(coef_level)
        diag_terms = diagonal(coef_pad, weight)
        extras = None
        field = single_sweeps(jnp.zeros_like(rhs_level), rhs_level, coef_pad, diag_terms, weight)
        residual = rhs_level - stencil(face_rim(field), coef_pad, weight)
        saved.append((field, rhs_level, coef_pad, diag_terms, weight, extras))
        rhs_level = restrict(residual)
        coef_level = restrict(coef_level)
    rows_x, rows_y, rows_z = rhs_level.shape
    stacked = jnp.stack([rhs_level, coef_level])[None]
    gathered = lax.all_gather(stacked, ("gy", "gz"), axis=0, tiled=True)
    slab = gathered.reshape(count_y, count_z, 2, rows_x, rows_y, rows_z)
    slab = slab.transpose(2, 3, 0, 4, 1, 5).reshape(2, rows_x, count_y * rows_y, count_z * rows_z)

    def lower_groups(rhs_low, coef_low):
        lowered = lax.all_gather(jnp.stack([rhs_low, coef_low]), "gx", axis=1, tiled=True)
        whole = coarse_solve(lowered[0], lowered[1])
        return lax.dynamic_slice_in_dim(whole, place_x * (rows_x // 2), rows_x // 2, 0)

    field = level_three(slab[0], slab[1], slab_pad, lower_groups)
    field = lax.dynamic_slice_in_dim(field, place_y * rows_y, rows_y, 1)
    result = lax.dynamic_slice_in_dim(field, place_z * rows_z, rows_z, 2)
    for level_index in (2, 1, 0):
        field, rhs_here, coef_pad, diag_terms, weight, extras = saved[level_index]
        field = field + prolong(result)
        field = single_sweeps(field, rhs_here, coef_pad, diag_terms, weight)
        result = field
    return result


ROWS = 48
MARGIN = 8
MAIN = MARGIN + 25 * ROWS + MARGIN
STRIP = MARGIN + 5 * ROWS + MARGIN
SECOND = MARGIN + 18 * ROWS + MARGIN


def roll(value, shift, axis):
    if isinstance(shift, int):
        shift = shift % value.shape[axis]
        if shift == 0:
            return value
    return pltpu.roll(value, shift, axis)


def iota(shape, axis):
    return lax.broadcasted_iota(jnp.int32, shape, axis)


def gather_lanes(value, lanes):
    return jnp.take_along_axis(value, lanes, axis=1, mode="promise_in_bounds")


def block(at, count):
    return pl.ds(pl.multiple_of(at, 8) if not isinstance(at, int) else at, count)


def terms(coef, nears, rhs, weight):
    faces = [0.5 * (coef + near) for near in nears]
    total = functools.reduce(lambda a, b: a + b, faces)
    scale = jnp.where(coef > 0.0, DAMPING / total, 0.0)
    return faces, scale, rhs * scale * (1.0 / weight), total * (weight / DAMPING)


def each(count, body, step):
    def several(turn, carry):
        for ahead in range(step):
            body(turn * step + ahead)
        return carry

    def single(index, carry):
        body(index)
        return carry

    whole = count // step
    lax.fori_loop(0, whole, several, 0)
    if count % step:
        lax.fori_loop(whole * step, count, single, 0)


def row_pairs(array, rows):
    return array[pl.ds(0, rows // 2, stride=2), :] + array[pl.ds(1, rows // 2, stride=2), :]


def repeat_rows(array, value):
    rows = value.shape[0]
    array[pl.ds(0, rows, stride=2), :] = value
    array[pl.ds(1, rows, stride=2), :] = value


def lane_pairs(value):
    return value + roll(value, -1, 1)


def both_ways(face, value, axis):
    return face * roll(value, -1, axis) + roll(face * value, 1, axis)


def by_side(swapped, odd):
    first, second = swapped
    return jnp.where(odd, first, second), jnp.where(odd, second, first)


def device_place():
    return [lax.axis_index(axis) for axis in ("gx", "gy", "gz")]


def odd_at(place, axis):
    return (place[axis] & 1) == 1


def with_tiles(middle, first, second, odd):
    sides = [by_side(tiles, odd) for tiles in zip(first, second)]
    return jnp.concatenate([low for low, _ in sides] + list(middle) + [high for _, high in sides], axis=0)


def main_at(plane):
    return MARGIN + ROWS * plane


def joined(middle, edge):
    lane = iota(middle.shape, 1)
    return jnp.where(lane == 127, edge, roll(middle, -1, 1)), jnp.where(lane == 0, edge, roll(middle, 1, 1))


def facing(own, plane, slot):
    lane = iota(own.shape, 1)
    return jnp.where((lane == 16 * slot + 7) | (lane == 16 * slot + 8), roll(plane, 16 * slot + 8, 1), own)


def strip_nears(strip, own, group):
    at = main_at(group + 1)
    middle = strip[block(at, ROWS)]
    lane = iota((ROWS, 128), 1)
    slot_lane = lane & 15
    further = jnp.where(lane < 112, roll(middle, -16, 1), roll(strip[block(at + ROWS, ROWS)], -16, 1))
    nearer = jnp.where(lane >= 16, roll(middle, 16, 1), roll(strip[block(at - ROWS, ROWS)], 16, 1))
    after = jnp.where(slot_lane == 7, own, roll(middle, -1, 1))
    before = jnp.where(slot_lane == 8, own, roll(middle, 1, 1))
    return middle, [further, nearer, roll(middle, -1, 0), roll(middle, 1, 0), after, before]


def finest_terms(rhs, coef, kept, inverse):
    main, strip = coef

    def group(index, slots):
        first = 8 * index + 1
        before = main[block(main_at(first - 1), ROWS)]
        here = main[block(main_at(first), ROWS)]
        held = strip[block(main_at(index + 1), ROWS)]
        own = jnp.zeros((ROWS, 128), jnp.float32)
        for slot in range(slots):
            at = block(main_at(first + slot), ROWS)
            after = main[block(main_at(first + slot + 1), ROWS)]
            nears = [after, before, roll(here, -1, 0), roll(here, 1, 0), *joined(here, roll(held, 120 - 16 * slot, 1))]
            faces, scale, start, back = terms(here, nears, rhs[0][at], 1.0)
            for side, value in enumerate((faces[0], faces[2], faces[4], faces[5], scale, start)):
                kept[0][side, at] = value
            inverse[at] = back
            own = facing(own, here, slot)
            before, here = here, after
        for slot in range(slots, 8):
            own = facing(own, main[block(main_at(first + slot), ROWS)], slot)
        at = block(main_at(index + 1), ROWS)
        middle, nears = strip_nears(strip, own, index)
        faces, scale, start, _ = terms(middle, nears, rhs[1][at], 1.0)
        for side in range(6):
            kept[1][side, at] = faces[side] * scale
        kept[1][6, at] = start

    each(2, lambda index: group(index, 8), 1)
    group(2, 6)


def finest_sweep(count, kept, source, target, keep=1.0 - DAMPING, strips=True):
    main, strip = source

    def group(index, slots):
        first = 8 * index + 1
        at = block(main_at(first - 1), ROWS)
        flux = kept[0][0, at] * main[at]
        here = main[block(main_at(first), ROWS)]
        held = strip[block(main_at(index + 1), ROWS)]
        own = jnp.zeros((ROWS, 128), jnp.float32)
        for slot in range(slots):
            at = block(main_at(first + slot), ROWS)
            after = main[block(main_at(first + slot + 1), ROWS)]
            face = kept[0][0, at]
            total = flux + face * after
            flux = face * here
            total = total + both_ways(kept[0][1, at], here, 0)
            above, below = joined(here, roll(held, 120 - 16 * slot, 1))
            total = total + kept[0][2, at] * above + kept[0][3, at] * below
            target[0][at] = kept[0][5, at] + keep * here + kept[0][4, at] * total
            if strips:
                own = facing(own, here, slot)
            here = after
        if strips:
            at = block(main_at(index + 1), ROWS)
            middle, nears = strip_nears(strip, own, index)
            total = kept[1][6, at] + keep * middle
            for side, near in enumerate(nears):
                total = total + kept[1][side, at] * near
            target[1][at] = total

    each(2, lambda index: group(index, 8), 1)
    if count > 16:
        group(2, count - 16)


def strip_pages(rhs_planes, coef_planes):
    lane = iota((32, 128), 1)
    left = jnp.zeros((32, 128), jnp.float32)
    right = jnp.zeros((32, 128), jnp.float32)
    for field_at, planes in ((0, rhs_planes), (8, coef_planes)):
        for slot, plane in enumerate(planes):
            at = 16 * slot + field_at
            inside = (lane >= at) & (lane < at + 8)
            left = jnp.where(inside, gather_lanes(plane, 7 - (lane & 7)), left)
            right = jnp.where(inside, gather_lanes(plane, 127 - (lane & 7)), right)
    return left, right


def pack_kernel(own, message, to_first, to_second, rows_first, rows_second):
    place = device_place()
    odd, odd_y = odd_at(place, 2), odd_at(place, 1)
    for group in range(2):
        planes = ([], [])
        for local in range(8 * group, 8 * group + 8):
            held = local + place[0] * (15 - 2 * local)
            for field_at in range(2):
                plane = own[16 * field_at + held]
                at = 16 * field_at + local
                rows_first[at], rows_second[at] = by_side((plane[0:8], plane[24:32]), odd_y)
                if local > 9 - field_at:
                    message[6 * field_at + 15 - local] = plane
                planes[field_at].append(plane)
        to_first[group], to_second[group] = by_side(strip_pages(*planes), odd)


def mirrored_slots(value):
    lane = iota(value.shape, 1)
    found = value
    for slot in range(8):
        inside = (lane >= 16 * slot) & (lane < 16 * slot + 16)
        found = jnp.where(inside, roll(value, 16 * (2 * slot - 7), 1), found)
    return found


def finest_kernel(own, strips, own_first, own_second, strip_first, strip_second, partner, beside, corner, pre, lower, message,
                  to_first, to_second, kept, kept_strip, rhs, rhs_strip, coef, coef_strip, va, va_strip, vb, vb_strip, inverse,
                  sums):
    place = device_place()
    blank = jnp.zeros((ROWS, 128), jnp.float32)
    outside = block(main_at(0), ROWS)
    for array in (coef, va, vb):
        array[outside] = blank
    coef[block(main_at(24), ROWS)] = blank
    kept[0, outside] = blank
    kept[5, outside] = blank
    for array in (coef_strip, va_strip, vb_strip, kept_strip.at[6]):
        array[outside] = blank
        array[block(main_at(4), ROWS)] = blank
    odd_y, odd_z = odd_at(place, 1), odd_at(place, 2)

    no_rows = jnp.zeros((8, 128), jnp.float32)
    for local in range(23):
        at = block(main_at(local + 1), ROWS)
        for field_at, array in enumerate((rhs, coef)):
            if local < 16:
                page = 16 * field_at + local
                held = 16 * field_at + local + place[0] * (15 - 2 * local)
                array[at] = with_tiles([own[held]], [own_first[page]], [own_second[page]], odd_y)
            elif local < 22 + field_at:
                step = local - 16
                page = 12 + 6 * field_at - step
                beyond = step == 5 + field_at
                first, second = (no_rows, no_rows) if beyond else (beside[page], beside[11 + page])
                array[at] = with_tiles([partner[6 * field_at + step]], [first], [second], odd_y)
    above = (iota((ROWS, 128), 1) & 15) < 8
    for group in range(3):
        pages = []
        for which in range(2):
            if group < 2:
                page = 2 - 2 * which + group
                pages.append(with_tiles([strips[page]], [strip_first[page]], [strip_second[page]], odd_y))
            else:
                tiles = [beside[4 - 4 * which + part] for part in range(4)]
                pages.append(with_tiles(tiles, [corner[1 - which]], [corner[3 - which]], odd_y))
        left, right = by_side(pages, odd_z)
        if group == 2:
            left, right = mirrored_slots(left), mirrored_slots(right)
        at = block(main_at(group + 1), ROWS)
        rhs_strip[at] = jnp.where(above, right, roll(left, 8, 1))
        coef_strip[at] = jnp.where(above, roll(right, -8, 1), left)
    both = (kept, kept_strip)
    finest_terms((rhs, rhs_strip), (coef, coef_strip), both, inverse)
    a, b = (va, va_strip), (vb, vb_strip)
    source = (kept.at[5], kept_strip.at[6])
    for count, target in zip(range(21, 16, -1), (a, b, a, b, a)):
        finest_sweep(count, both, source, target)
        source = target
    finest_sweep(16, both, a, b, -DAMPING, False)

    def pair(index):
        total = jnp.zeros((32, 128), jnp.float32)
        conduct = jnp.zeros((32, 128), jnp.float32)
        for local in (2 * index, 2 * index + 1):
            at = block(main_at(local + 1) + 8, 32)
            value = va[at]
            pre[local] = value
            total = total + vb[at] * inverse[at]
            conduct = conduct + coef[at]
        sums[block(index * 32, 32)] = total
        sums[block(index * 32 + 256, 32)] = conduct

    each(8, pair, 4)
    folded = lane_pairs(row_pairs(sums, 512)) * 0.125
    lane = iota((128, 128), 1)
    merged = jnp.where(lane < 64, gather_lanes(folded[0:128], (2 * lane) & 127), gather_lanes(folded[128:256], (2 * lane) & 127))
    lane = iota((16, 128), 1)
    for group in range(2):
        right = jnp.zeros((16, 128), jnp.float32)
        left = jnp.zeros((16, 128), jnp.float32)
        for slot in range(4):
            local = 4 * group + slot
            plane = merged[16 * local : 16 * local + 16]
            lower[local] = plane
            message[2 * local] = plane[0:8]
            message[2 * local + 1] = plane[8:16]
            for field_at in range(2):
                at = 32 * slot + 16 * field_at
                inside = (lane >= at) & (lane < at + 16)
                right = jnp.where(inside, roll(plane, at - 48 - 64 * field_at, 1), right)
                left = jnp.where(inside, roll(plane, at - 64 * field_at, 1), left)
        rows = slice(16 * group, 16 * group + 16)
        to_first[rows], to_second[rows] = by_side((left, right), odd_z)
    lane = iota((32, 128), 1)
    mirrored = jnp.where((lane & 15) < 8, 7 - (lane & 15), 135 - (lane & 15))
    for local in range(10, 16):
        for part in range(4):
            message[4 * local - 24 + part] = pre[local, 8 * part : 8 * part + 8]
    for group in range(2):
        value = jnp.zeros((32, 128), jnp.float32)
        for slot in range(8):
            inside = (lane >= 16 * slot) & (lane < 16 * slot + 16)
            value = jnp.where(inside, gather_lanes(pre[8 * group + slot], mirrored), value)
        rows = slice(64 - 32 * group, 96 - 32 * group)
        to_first[rows] = value
        to_second[rows] = value


def second_window(place, own, first, second, rhs, coef):
    lane = iota((ROWS, 128), 1)
    odd_y, odd_z = odd_at(place, 1), odd_at(place, 2)

    def page(index):
        low, high = by_side((first[2 * index], second[2 * index]), odd_y)
        low_next, high_next = by_side((first[2 * index + 1], second[2 * index + 1]), odd_y)
        return jnp.concatenate([low, low_next, own[index], high, high_next], axis=0)

    for group in range(4):
        at = (8 + group) if group < 2 else 18 + group
        left, right = by_side((page(at), page(at + 2)), odd_z)
        for slot in range(4):
            other = 4 * group + slot
            local, middle = (other, page(other)) if group < 2 else (23 - other, page(4 + other))
            for field_at, array in enumerate((rhs, coef)):
                at = 32 * slot + 16 * field_at
                value = jnp.where(lane < 64, roll(middle, -64 * field_at, 1), 0.0)
                value = jnp.where((lane >= 64) & (lane < 80), roll(right, 64 - at, 1), value)
                array[block(main_at(local + 1), ROWS)] = jnp.where(lane >= 112, roll(left, 112 - at, 1), value)


def second_sweep(count, kept, source, target, skip=0, keep=1.0 - DAMPING):
    rows = ROWS - 2 * skip
    at = block(main_at(0) + skip, rows)
    flux = kept[0, at] * source[at]
    here = source[block(main_at(1) + skip, rows)]
    for plane in range(1, count + 1):
        at = block(main_at(plane) + skip, rows)
        after = source[block(main_at(plane + 1) + skip, rows)]
        face = kept[0, at]
        total = flux + face * after
        flux = face * here
        total = total + both_ways(kept[1, at], here, 0) + both_ways(kept[2, at], here, 1)
        target[at] = kept[4, at] + keep * here + kept[3, at] * total
        here = after


def second_kernel(own, first, second, share, va, kept, rhs, coef, inverse, vb, sums):
    place = device_place()
    blank = jnp.zeros((ROWS, 128), jnp.float32)
    for plane in (0, 17):
        at = block(main_at(plane), ROWS)
        for array in (coef, va, vb, kept.at[0], kept.at[4]):
            array[at] = blank
    second_window(place, own, first, second, rhs, coef)

    def plane(index):
        at = block(main_at(index + 1), ROWS)
        here = coef[at]
        nears = [coef[block(main_at(index + 2), ROWS)], coef[block(main_at(index), ROWS)],
                 roll(here, -1, 0), roll(here, 1, 0), roll(here, -1, 1), roll(here, 1, 1)]
        faces, scale, start, inverse[at] = terms(here, nears, rhs[at], 0.25)
        for side, value in enumerate((faces[0], faces[2], faces[4], scale, start)):
            kept[side, at] = value

    each(16, plane, 4)
    second_sweep(16, kept, kept.at[4], va)

    def twice(index, carry):
        second_sweep(16, kept, va, vb)
        second_sweep(16, kept, vb, va)
        return carry

    lax.fori_loop(0, 2, twice, 0)
    second_sweep(16, kept, va, vb, 8, -DAMPING)
    for local in range(8):
        residual = jnp.zeros((16, 128), jnp.float32)
        conduct = jnp.zeros((16, 128), jnp.float32)
        for here in (2 * local + 1, 2 * local + 2):
            at = block(main_at(here) + 16, 16)
            residual = residual + vb[at] * inverse[at]
            conduct = conduct + coef[at]
        sums[16 * local : 16 * local + 16] = residual
        sums[128 + 16 * local : 144 + 16 * local] = conduct
    folded = lane_pairs(row_pairs(sums, 256)) * 0.125
    lane = iota((8, 128), 1)
    for group in range(4):
        value = jnp.zeros((8, 128), jnp.float32)
        for plane in range(2):
            for field_at in range(2):
                row = 64 * field_at + 8 * (2 * group + plane)
                at = 64 * plane + 32 * field_at
                inside = (lane >= at) & (lane < at + 32)
                value = jnp.where(inside, gather_lanes(folded[row : row + 8], (2 * lane) & 63), value)
        for device in range(share.shape[0]):
            share[device, group] = value


def whole_terms(planes, rows, lanes, rhs, coef, kept, weight):
    row = iota((rows, 128), 0)
    lane = iota((rows, 128), 1)
    outside = jnp.zeros((rows, 128), jnp.float32)
    held = [outside] + [coef[here] for here in range(planes)] + [outside]
    for here in range(planes):
        middle = held[here + 1]
        nears = [
            held[here + 2], held[here],
            jnp.where(row == rows - 1, 0.0, roll(middle, -1, 0)), jnp.where(row == 0, 0.0, roll(middle, 1, 0)),
            jnp.where(lane >= lanes - 1, 0.0, roll(middle, -1, 1)), jnp.where(lane == 0, 0.0, roll(middle, 1, 1))]
        faces, scale, start, back = terms(middle, nears, rhs[here], weight)
        for side in range(3):
            kept[side, here] = jnp.where(nears[2 * side] > 0.0, faces[2 * side], 0.0)
        kept[3, here] = scale
        kept[4, here] = start
        kept[5, here] = back


def whole_change(kept, values, keep):
    found = []
    flux = None
    for here, value in enumerate(values):
        total = both_ways(kept[1, here], value, 0) + both_ways(kept[2, here], value, 1)
        if here > 0:
            total = total + flux
        if here + 1 < len(values):
            face = kept[0, here]
            total = total + face * values[here + 1]
            flux = face * value
        found.append(kept[4, here] + keep * value + kept[3, here] * total)
    return tuple(found)


def whole_sweeps(count, kept, values):
    return lax.fori_loop(0, count, lambda index, held: whole_change(kept, held, 1.0 - DAMPING), tuple(values))


def whole_solve(level, scratch):
    kept, rhs, coef, rows_of = scratch[0]
    planes, rows = rhs.shape[0], rhs.shape[1]
    lanes = 128 >> (level - 2)
    whole_terms(planes, rows, lanes, rhs, coef, kept, 0.25**level)
    start = [kept[4, here] for here in range(planes)]
    values = whole_sweeps((COARSE_SWEEPS if level == 4 else SWEEPS) - 1, kept, start)
    if level < 4:
        residual = [value * kept[5, here] for here, value in enumerate(whole_change(kept, values, -DAMPING))]
        size = planes // 2 * rows
        for pair in range(planes // 2):
            at = pair * rows
            rows_of[at : at + rows] = residual[2 * pair] + residual[2 * pair + 1]
            rows_of[size + at : size + at + rows] = coef[2 * pair] + coef[2 * pair + 1]
        folded = lane_pairs(row_pairs(rows_of, 2 * size)) * 0.125
        lane = iota(folded.shape, 1)
        folded = jnp.where(lane < lanes // 2, gather_lanes(folded, (2 * lane) & 127), 0.0)
        half = rows // 2
        for pair in range(planes // 2):
            scratch[1][1][pair] = folded[pair * half : pair * half + half]
            scratch[1][2][pair] = folded[size // 2 + pair * half : size // 2 + pair * half + half]
        lower = jnp.concatenate(whole_solve(level + 1, scratch[1:]), axis=0)
        repeat_rows(rows_of.at[0:size], gather_lanes(lower, lax.shift_right_logical(iota(lower.shape, 1), 1)))
        values = [
            value + rows_of[here // 2 * rows : here // 2 * rows + rows] for here, value in enumerate(values)]
        values = whole_sweeps(SWEEPS, kept, values)
    return list(values)


def whole_scratch(planes, rows):
    return [field(6, planes, rows, 128), field(planes, rows, 128), field(planes, rows, 128), field(planes * rows, 128)]


def third_whole(shares, count_y, count_z, rhs, coef):
    lane = iota((8, 128), 1)
    width = 128 // count_z
    for local in range(8):
        for at_y in range(count_y):
            for index, array in enumerate((rhs, coef)):
                value = jnp.zeros((8, 128), jnp.float32)
                for at_z in range(count_z):
                    held = shares[at_y * count_z + at_z, local // 2]
                    at = 64 * (local % 2) + 32 * index
                    inside = (lane >= width * at_z) & (lane < width * at_z + width)
                    value = jnp.where(inside, roll(held, width * at_z - at, 1), value)
                array[local, 8 * at_y : 8 * at_y + 8] = value


def last_kernel(count_y, count_z, own2, first1, second1, shares, pre1, kept1, kept, kept_strip, out, *scratch):
    place = device_place()
    deep = [scratch[0:4], scratch[4:8], scratch[8:12]]
    va1, vb1, va, va_strip, vb, vb_strip = scratch[12:18]
    framed, twice1, twice0 = scratch[18:21]
    third_whole(shares, count_y, count_z, deep[0][1], deep[0][2])
    third = whole_solve(2, deep)

    blank = jnp.zeros((ROWS, 128), jnp.float32)
    for array, outer in ((va1, 17), (va_strip, 4), (vb_strip, 4)):
        array[block(main_at(outer), ROWS)] = blank
    for array in (va1, va, va_strip, vb, vb_strip):
        array[block(main_at(0), ROWS)] = blank
    rows = third[0].shape[0]
    for index, plane in enumerate(third):
        framed[index, 0:8] = blank[0:8]
        framed[index, 8 : 8 + rows] = plane
        framed[index, 8 + rows : 16 + rows] = blank[0:8]
    for index in range(8):
        near = framed[index, pl.ds(pl.multiple_of(8 * place[1], 8), 24), :]
        repeat_rows(twice1.at[48 * index : 48 * index + 48], near)
    lane = iota((ROWS, 128), 1)
    held = lax.shift_right_arithmetic(jnp.where(lane < 96, lane, lane - 128), 1) + 32 * place[2]
    inside = (held >= 0) & (held < 128) & ((lane < 80) | (lane >= 112))
    for index in range(8):
        wide = jnp.where(inside, gather_lanes(twice1[48 * index : 48 * index + 48], held & 127), 0.0)
        for here in (2 * index + 1, 2 * index + 2):
            there = block(main_at(here), ROWS)
            va1[there] = pre1[there] + jnp.where(kept1[3, there] > 0.0, wide, 0.0)
    vb1[block(main_at(0), ROWS)] = blank
    vb1[block(main_at(17), ROWS)] = blank
    source, target = va1, vb1
    for sweep in range(SWEEPS):
        second_sweep(16 - sweep, kept1, source, target, 8 if sweep else 0)
        source, target = target, source

    odd_y = odd_at(place, 1)

    def page(index):
        low, high = by_side((first1[48 + index], second1[48 + index]), odd_y)
        return jnp.concatenate([low, own2[index], high], axis=0)

    slot_lane = lane & 15
    above = slot_lane < 8
    facing_lane = jnp.where(above, 64 + lax.shift_right_logical(7 - slot_lane, 1), 127 - lax.shift_right_logical(slot_lane - 8, 1))
    for group in range(3):
        more = jnp.zeros((ROWS, 128), jnp.float32)
        for index in range(4 * group, min(4 * group + 4, 11)):
            at = main_at(index + 1) + 8
            repeat_rows(twice0, source[at : at + 32])
            near = twice0[8:56]
            wide = gather_lanes(near, lax.shift_right_logical(lane, 1))
            at = 32 * (index - 4 * group)
            more = jnp.where((lane >= at) & (lane < at + 32), gather_lanes(near, facing_lane & 127), more)
            for local in (2 * index, 2 * index + 1):
                there = block(main_at(local + 1), ROWS)
                middle = page(local if local < 16 else 39 - local)
                va[there] = middle + jnp.where(kept[4, there] > 0.0, wide, 0.0)
        value = mirrored_slots(page(24)) if group == 2 else page(17 - group)
        there = block(main_at(group + 1), ROWS)
        va_strip[there] = value + jnp.where(kept_strip[0, there] > 0.0, more, 0.0)
    source, target = (va, va_strip), (vb, vb_strip)
    for count in range(21, 15, -1):
        finest_sweep(count, (kept, kept_strip), source, target, strips=count > 16)
        source, target = target, source

    def leave(local):
        out[local + place[0] * (15 - 2 * local)] = source[0][block(main_at(local + 1) + 8, 32)]

    each(16, leave, 4)


def call(kernel, inputs, outs, scratch):
    near = pl.BlockSpec(memory_space=pltpu.VMEM)
    return pl.pallas_call(
        kernel,
        out_shape=[jax.ShapeDtypeStruct(shape, jnp.float32) for shape in outs],
        in_specs=[near] * len(inputs),
        out_specs=[near] * len(outs),
        scratch_shapes=scratch,
        compiler_params=pltpu.CompilerParams(vmem_limit_bytes=VMEM_BYTES),
    )(*inputs)


def field(*shape):
    return pltpu.VMEM(shape, jnp.float32)


def from_sides(axis, to_first, to_second):
    size = lax.axis_size(axis)
    found = []
    for message, begin in ((to_second, 1), (to_first, 0)):
        lower = [(i, i + 1) for i in range(begin, size - 1, 2)]
        found.append(lax.ppermute(message, axis, lower + [(j, i) for i, j in lower]))
    return found[::-1]


def edge_rows(array, axis, last):
    odd = lax.axis_index(axis) % 2
    rows = array.shape[1]
    return lax.dynamic_slice_in_dim(array, (rows - 8) * (odd if last else 1 - odd), 8, 1)


def from_partner(message):
    return lax.ppermute(message, "gx", [(0, 1), (1, 0)])


def merged_sides(first, second):
    odd = lax.axis_index("gz") % 2 == 1
    above = lax.broadcasted_iota(jnp.int32, (128,), 0) % 16 < 8
    return jnp.where(above == odd, second, first)


def fast_shards(source, conductivity):
    count_y, count_z = lax.axis_size("gy"), lax.axis_size("gz")
    second = lax.broadcasted_iota(jnp.int32, (2, *source.shape), 0) == 1
    own = jnp.where(second, conductivity[None], source[None]).reshape(32, 32, 128)
    message, to_first, to_second, *rows = call(
        pack_kernel,
        (own,),
        [(13, 32, 128), (2, 32, 128), (2, 32, 128), (32, 8, 128), (32, 8, 128)],
        [])
    partner = from_partner(message)
    strips = jnp.concatenate(from_sides("gz", to_first, to_second)[::-1])
    own_rev = from_sides("gy", *rows)[::-1]
    own_rev = lax.optimization_barrier(own_rev)
    own_rows = own_rev[::-1]
    strip_rows = from_sides("gy", *(edge_rows(strips, "gy", last) for last in (False, True)))
    message = jnp.concatenate(
        [strips[1].reshape(4, 8, 128), strips[3].reshape(4, 8, 128)]
        + [part for array in own_rows for part in (array[11:16], array[26:32])])
    beside = from_partner(message)
    strip_rows, _ = lax.optimization_barrier((strip_rows, message))
    corner = from_partner(jnp.concatenate([array[at : at + 1] for array in strip_rows for at in (1, 3)]))

    main, strip = field(MAIN, 128), field(STRIP, 128)
    kept = [(6, MAIN, 128), (7, STRIP, 128)]
    pre, lower, message, to_first, to_second, *kept0 = call(
        finest_kernel,
        (own, strips, *own_rows, *strip_rows, partner, beside, corner),
        [(16, 32, 128), (8, 16, 128), (40, 8, 128), (96, 128), (96, 128), *kept],
        [main, strip] * 4 + [main, field(512, 128)])
    partner = from_partner(message)
    strips = from_sides("gz", to_first, to_second)
    lower_strips = jnp.concatenate([part[:32].reshape(4, 8, 128) for part in strips])
    pre_strips = merged_sides(*(part[32:].reshape(2, 32, 128) for part in strips))
    further = from_partner(jnp.concatenate([lower_strips, pre_strips[0].reshape(4, 8, 128)]))
    flat = jnp.concatenate([lower.reshape(16, 8, 128), lower_strips, partner[:16], further[:8]])
    own2 = jnp.concatenate([pre, pre_strips, partner[16:].reshape(6, 32, 128), further[8:].reshape(1, 32, 128)])
    rows1 = from_sides("gy", *(jnp.concatenate([flat, edge_rows(own2, "gy", last)]) for last in (False, True)))

    window = field(SECOND, 128)
    share, *kept1 = call(
        second_kernel,
        (flat.reshape(24, 16, 128), *rows1),
        [(count_y * count_z, 4, 8, 128), (SECOND, 128), (5, SECOND, 128)],
        [window] * 4 + [field(256, 128)])
    shares = lax.all_to_all(share, ("gy", "gz"), 0, 0, tiled=True)

    scratch = whole_scratch(8, 32) + whole_scratch(4, 16) + whole_scratch(2, 8)
    scratch += [window, window] + [main, strip] * 2 + [field(8, 48, 128), field(384, 128), field(64, 128)]
    (result,) = call(
        functools.partial(last_kernel, count_y, count_z),
        (own2, *rows1, shares, *kept1, *kept0),
        [(16, 32, 128)],
        scratch)
    return result


def solution(mesh):
    in_specs = (P("gx", "gy", "gz"), P("gx", "gy", "gz"))
    out_specs = P("gx", "gy", "gz")

    def run(source, conductivity):
        counts = tuple(mesh.shape[axis] for axis in ("gx", "gy", "gz"))
        held = tuple(size // count for size, count in zip(source.shape, counts))
        fast = counts == (2, 4, 4) and held == (16, 32, 128)
        shards = fast_shards if fast else plain_shards
        return jax.shard_map(shards, mesh=mesh, in_specs=in_specs, out_specs=out_specs, check_vma=False)(source, conductivity)

    return run
```
